32 devices in a mesh: seq: 8 (over z, y), head: 4 (over x, core).
Axes of the slice: x: 2, y: 2, z: 4, core: 2. Of those that a mesh axis runs over, the one named last changes fastest.
Arguments:
- frames: bfloat16 [24576, 8192], P('seq', 'head'), may hold values from -6 to 6
- state_proj: bfloat16 [256, 24576], P('head', 'seq'), as said below
- log_decay: float32 [128, 24576], P('head', 'seq'), may hold values from -0.7 to 0
- skip_gain: float32 [128], P('head'), may hold values from 0.1 to 1.9
- group_pos: int32 [96], P('seq'), may hold values from 0 to 95, as said below
Outputs:
- mixed: bfloat16 [24576, 8192], P('seq', 'head')
The draws below stay inside these ranges and needn't reach their ends.
Inputs may be any that keep to these rules, and one draw needn't show every extreme that they name: `group_pos`: device d of seq holds in its 12 slots the groups of sequence positions d * 12 to (d + 1) * 12 - 1, each once, in an order drawn from the seed. `state_proj`: entries lie within 5 times their scale, which is the inverse fourth root of 393216.
All inputs are finite; a program needn't handle non-finite values.
Results may differ from the reference program's by a relative error of at most 0.0053.
Values may be sent and summed in bfloat16 or wider, within the bound.
A program may use at most 128 MiB of HBM per device.

```python
import jax
import jax.numpy as jnp
from jax import lax

HEADS = 128
HEAD_DIM = 64
STATE = 128
GROUP = 256
CH_DEV = 12
GROUPS = 96
SAMPLE_COUNT = 24576


def draw_state_proj(key, part):
    spread = float(STATE * CH_DEV * GROUP) ** (-0.25)
    values = jnp.clip(jax.random.normal(key, (2 * STATE, SAMPLE_COUNT), jnp.float32), -5.0, 5.0)
    return (values * spread).astype(jnp.bfloat16)


def draw_log_decay(key, part):
    lookup_entries = jax.random.split(key, 5)
    pick = jax.random.uniform(lookup_entries[0], (HEADS,), jnp.float32)
    low = jnp.log(0.005 / SAMPLE_COUNT)
    high = jnp.log(0.03)
    rate_head = jnp.exp(low + pick * (high - low))
    reset_keys = jax.random.split(jax.random.fold_in(key, 7001), 6)
    reset_order = jax.random.permutation(reset_keys[0], HEADS)
    reset_head = reset_order < HEADS // 4
    memory_pick = jax.random.uniform(reset_keys[1], (HEADS,), jnp.float32)
    memory_low = jnp.log(0.2 / SAMPLE_COUNT)
    memory_high = jnp.log(2.0 / SAMPLE_COUNT)
    memory_rate = jnp.exp(memory_low + memory_pick * (memory_high - memory_low))
    rate_head = jnp.where(reset_head, memory_rate, rate_head)
    rough = jax.random.uniform(lookup_entries[1], (HEADS, SAMPLE_COUNT), jnp.float32, 0.5, 2.0)
    block_multiplier = jax.random.uniform(lookup_entries[2], (GROUPS,), jnp.float32, 0.5, 2.0)
    block_rows = jnp.repeat(block_multiplier, GROUP)
    natlog_speeds = -rate_head[:, None] * rough * block_rows[None, :]
    packet_span = jax.random.uniform(lookup_entries[3], (SAMPLE_COUNT,), jnp.float32) < 6.0 / SAMPLE_COUNT
    network_level = jax.random.uniform(lookup_entries[4], (HEADS, SAMPLE_COUNT), jnp.float32, 0.22, 0.69)
    shaped = jnp.where(packet_span[None, :], -network_level, natlog_speeds)
    blocks = GROUPS // CH_DEV
    reset_device = jax.random.randint(reset_keys[2], (), blocks // 2, blocks - 1)
    reset_slot = jax.random.randint(reset_keys[3], (), 0, CH_DEV)
    reset_offset = jax.random.randint(reset_keys[4], (), 0, GROUP - 8 + 1)
    reset_start = (reset_device * CH_DEV + reset_slot) * GROUP + reset_offset
    columns = jnp.arange(SAMPLE_COUNT, dtype=jnp.int32)
    reset_cols = (columns >= reset_start) & (columns < reset_start + 8)
    deep_level = jax.random.uniform(reset_keys[5], (HEADS, SAMPLE_COUNT), jnp.float32, 0.6, 0.69)
    deep_mask = reset_head[:, None] & reset_cols[None, :]
    return jnp.where(deep_mask, -deep_level, shaped).astype(jnp.float32)


def draw_group_pos(key, part):
    blocks = GROUPS // CH_DEV
    lookup_entries = jax.random.split(key, blocks)
    orders = jax.vmap(lambda block_key_rows: jax.random.permutation(block_key_rows, CH_DEV))(lookup_entries)
    offsets = jnp.arange(blocks, dtype=jnp.int32)[:, None] * CH_DEV
    return (orders.astype(jnp.int32) + offsets).reshape(-1).astype(jnp.int32)


def shard_levels(own_key, shape, shards, smallest, largest):
    def one(axis_at, parts):
        steps = jax.random.uniform(jax.random.fold_in(jax.random.fold_in(own_key, 6), axis_at), (parts,), jnp.float32, smallest / len(shards), largest / len(shards))
        return jnp.repeat(jnp.exp(steps), shape[axis_at] // parts).reshape((-1,) + (1,) * (len(shape) - axis_at - 1))

    gain = one(*shards[0])
    for cut in shards[1:]:
        gain = gain * one(*cut)
    return gain


def gaussian(own_key, dims, width, limit, cuts=(), kind=jnp.bfloat16):
    entries = jax.random.normal(own_key, dims, jnp.float32) * width
    if len(cuts) > 0:
        entries = shard_levels(own_key, dims, cuts, -0.22, 0.18) * entries
    return jnp.clip(entries, min=-limit, max=limit).astype(kind)


def setup_inputs(seed: int = 0) -> dict:
    splits = jax.random.split(jax.random.key(seed), 6)
    return {
        "frames": gaussian(splits[0], (SAMPLE_COUNT, HEADS * HEAD_DIM), 1.0, 6.0, ((0, 8), (1, 4))),
        "state_proj": draw_state_proj(jax.random.fold_in(splits[5], 71), 0),
        "log_decay": draw_log_decay(jax.random.fold_in(splits[5], 71), 0),
        "skip_gain": jnp.clip(1.0 + 0.18 * jax.random.normal(splits[3], (HEADS,), jnp.float32), 0.1, 1.9),
        "group_pos": draw_group_pos(jax.random.fold_in(splits[5], 71), 0),
    }


def group_terms(inputs, group_in, natlog_speeds):
    running = jnp.cumsum(natlog_speeds, axis=1)
    input_map = group_in[:STATE]
    output_map = group_in[STATE:]
    coupling = jnp.dot(output_map.T, input_map, preferred_element_type=jnp.float32)
    step_ids = jnp.arange(running.shape[1])
    causal = (step_ids[:, None] >= step_ids[None, :])[None]
    log_gap = running[:, :, None] - running[:, None, :]
    decay_table = jnp.where(causal, jnp.exp(jnp.where(causal, log_gap, 0.0)), 0.0)
    weights = lax.optimization_barrier((coupling[None] * decay_table).astype(jnp.bfloat16))
    within = jnp.einsum("hts,shp->thp", weights.astype(jnp.float32), inputs.astype(jnp.float32))
    group_log = running[:, -1]
    carried = lax.optimization_barrier((inputs.astype(jnp.float32) * jnp.exp(group_log[:, None] - running).T[:, :, None]).astype(jnp.bfloat16))
    summary = jnp.einsum("shp,ns->hpn", carried.astype(jnp.float32), input_map.astype(jnp.float32))
    return within, summary, running


def reference(frames, state_proj, log_decay, skip_gain, group_pos):
    group_count = group_pos.shape[0]
    inverse = jnp.zeros((group_count,), jnp.int32).at[group_pos].set(jnp.arange(group_count, dtype=jnp.int32))
    frames_seq = frames.reshape(group_count, GROUP, HEADS, HEAD_DIM)[inverse]
    proj_seq = state_proj.reshape(2 * STATE, group_count, GROUP).transpose(1, 0, 2)[inverse]
    decay_seq = log_decay.reshape(HEADS, group_count, GROUP).transpose(1, 0, 2)[inverse]

    def advance(carry_state, group_item):
        inputs, group_in, natlog_speeds = group_item
        within, summary, running = group_terms(inputs, group_in, natlog_speeds)
        held_state = lax.optimization_barrier(carry_state.astype(jnp.bfloat16))
        output_map = group_in[STATE:]
        across_shards = jnp.einsum("hpn,nt->thp", held_state.astype(jnp.float32), output_map.astype(jnp.float32))
        across_shards = across_shards * jnp.exp(running).T[:, :, None]
        output = (within + across_shards + skip_gain[None, :, None] * inputs.astype(jnp.float32)).astype(jnp.bfloat16)
        carry_state = jnp.exp(running[:, -1])[:, None, None] * carry_state + summary
        return carry_state, output

    empty_state = jnp.zeros((HEADS, HEAD_DIM, STATE), jnp.float32)
    _, outputs = lax.scan(advance, empty_state, (frames_seq, proj_seq, decay_seq))
    return outputs.reshape(group_count * GROUP, HEADS * HEAD_DIM)
```

```python
import functools

import jax
import jax.numpy as jnp
from jax import lax
from jax.experimental import pallas as pl
from jax.experimental.pallas import tpu as pltpu
from jax.sharding import PartitionSpec as P

HEAD_DIM = 64
STATE = 128
GROUP = 256
CHUNK = 128
TILE = 256
VMEM_BYTES = 48 * 1024 * 1024


def spread_matrix(heads, columns):
    rows = lax.broadcasted_iota(jnp.int32, (2 * heads, columns), 0) % heads
    owner = lax.broadcasted_iota(jnp.int32, (2 * heads, columns), 1) // HEAD_DIM
    return (rows == owner).astype(jnp.float32).astype(jnp.bfloat16)


def lower_matrix(length):
    rows = lax.broadcasted_iota(jnp.int32, (length, length), 0)
    columns = lax.broadcasted_iota(jnp.int32, (length, length), 1)
    return rows >= columns


def running_sums(logs, lower):
    twice = jnp.concatenate([logs, logs], axis=0)
    high = twice.astype(jnp.bfloat16)
    rest = twice - high.astype(jnp.float32)
    middle = rest.astype(jnp.bfloat16)
    low = (rest - middle.astype(jnp.float32)).astype(jnp.bfloat16)
    total = None
    for term in (low, middle, high):
        part = lax.dot_general(
            lower, term, (((1,), (1,)), ((), ())), preferred_element_type=jnp.float32
        )
        total = part if total is None else total + part
    return total


def two_terms(values, heads):
    high = values.astype(jnp.bfloat16).astype(jnp.float32)
    lanes = lax.broadcasted_iota(jnp.int32, values.shape, 1)
    return jnp.where(lanes < heads, high, values - high).astype(jnp.bfloat16)


def summary_kernel(x_ref, proj_ref, log_ref, after_ref, out_ref, acc_ref, spread_ref):
    step = pl.program_id(0)
    heads = log_ref.shape[0]
    columns = x_ref.shape[1]

    @pl.when(step == 0)
    def _():
        acc_ref[...] = jnp.zeros_like(acc_ref)
        spread_ref[...] = spread_matrix(heads, columns)

    lower = lower_matrix(GROUP).astype(jnp.float32).astype(jnp.bfloat16)
    running = running_sums(log_ref[...], lower)
    decay = two_terms(jnp.exp(after_ref[0] - running), heads)
    for start in range(0, columns, TILE):
        tile = slice(start, start + TILE)
        wide = jnp.dot(decay, spread_ref[:, tile], preferred_element_type=jnp.float32)
        carried = (x_ref[:, tile].astype(jnp.float32) * wide).astype(jnp.bfloat16)
        acc_ref[:, tile] += jnp.dot(proj_ref[...], carried, preferred_element_type=jnp.float32)

    @pl.when(step == pl.num_programs(0) - 1)
    def _():
        out_ref[...] = acc_ref[...].astype(out_ref.dtype)


def summarise(frames, proj, logs, after):
    frame_count, columns = frames.shape
    heads = logs.shape[0]
    groups = frame_count // GROUP
    return pl.pallas_call(
        summary_kernel,
        grid=(groups,),
        in_specs=[
            pl.BlockSpec((GROUP, columns), lambda i: (i, 0)),
            pl.BlockSpec((STATE, GROUP), lambda i: (0, i)),
            pl.BlockSpec((heads, GROUP), lambda i: (0, i)),
            pl.BlockSpec((1, 1, 2 * heads), lambda i: (i, 0, 0)),
        ],
        out_specs=pl.BlockSpec((STATE, columns), lambda i: (0, 0)),
        out_shape=jax.ShapeDtypeStruct((STATE, columns), jnp.bfloat16),
        scratch_shapes=[
            pltpu.VMEM((STATE, columns), jnp.float32),
            pltpu.VMEM((2 * heads, columns), jnp.bfloat16),
        ],
        compiler_params=pltpu.CompilerParams(vmem_limit_bytes=VMEM_BYTES),
        cost_estimate=pl.CostEstimate(
            flops=4 * frame_count * columns * STATE,
            bytes_accessed=2 * frame_count * columns,
            transcendentals=frame_count * heads,
        ),
        name="summary",
    )(frames, proj, logs, after)


def mix_kernel(
    slot_ref, x_ref, proj_ref, log_ref, skip_ref, enter_ref, out_ref, state_ref, spread_ref, both_ref
):
    step = pl.program_id(0)
    heads = log_ref.shape[0]
    columns = x_ref.shape[1]

    @pl.when(step == 0)
    def _():
        state_ref[...] = enter_ref[...].astype(jnp.float32)
        spread_ref[...] = spread_matrix(heads, columns)

    causal = lower_matrix(CHUNK)
    lower = causal.astype(jnp.float32).astype(jnp.bfloat16)
    half = CHUNK // 2
    for first in range(0, GROUP, CHUNK):
        rows = slice(first, first + CHUNK)
        running = running_sums(log_ref[:, rows], lower)
        middle = running[half - 1 : half]
        last = running[CHUNK - 1 : CHUNK]
        extra = lax.broadcasted_iota(jnp.int32, (16, 2 * heads), 0)
        exponents = jnp.concatenate(
            [middle - running, running - middle, jnp.where(extra == 0, middle, last - middle)], axis=0
        )
        decay = two_terms(jnp.exp(exponents), heads)
        input_map = proj_ref[:STATE, rows]
        output_map = proj_ref[STATE:, rows].astype(jnp.float32).T.astype(jnp.bfloat16)
        coupling = jnp.dot(output_map, input_map, preferred_element_type=jnp.float32)
        coupling = jnp.where(causal, coupling, 0.0).astype(jnp.bfloat16)
        left = jnp.concatenate([coupling, output_map], axis=1)
        for start in range(0, columns, TILE):
            tile = slice(start, start + TILE)
            wide = jnp.dot(decay, spread_ref[:, tile], preferred_element_type=jnp.float32)
            x = x_ref[rows, tile].astype(jnp.float32)
            scaled = (x * wide[:CHUNK]).astype(jnp.bfloat16)
            prior = state_ref[:, tile] * wide[2 * CHUNK : 2 * CHUNK + 1]
            both_ref[:CHUNK, tile] = scaled
            both_ref[CHUNK:, tile] = prior.astype(jnp.bfloat16)
            mixed = jnp.dot(left, both_ref[:, tile], preferred_element_type=jnp.float32)
            out_ref[rows, tile] = (
                mixed * wide[CHUNK : 2 * CHUNK] + skip_ref[:, tile] * x
            ).astype(out_ref.dtype)
            update = jnp.dot(input_map, scaled, preferred_element_type=jnp.float32)
            state_ref[:, tile] = (prior + update) * wide[2 * CHUNK + 1 : 2 * CHUNK + 2]


def mix(slots, frames, proj, logs, skip, entering):
    frame_count, columns = frames.shape
    heads = logs.shape[0]
    groups = frame_count // GROUP
    grid_spec = pltpu.PrefetchScalarGridSpec(
        num_scalar_prefetch=1,
        grid=(groups,),
        in_specs=[
            pl.BlockSpec((GROUP, columns), lambda i, slot: (slot[i], 0)),
            pl.BlockSpec((2 * STATE, GROUP), lambda i, slot: (0, slot[i])),
            pl.BlockSpec((heads, GROUP), lambda i, slot: (0, slot[i])),
            pl.BlockSpec((1, columns), lambda i, slot: (0, 0)),
            pl.BlockSpec((STATE, columns), lambda i, slot: (0, 0)),
        ],
        out_specs=pl.BlockSpec((GROUP, columns), lambda i, slot: (i, 0)),
        scratch_shapes=[
            pltpu.VMEM((STATE, columns), jnp.float32),
            pltpu.VMEM((2 * heads, columns), jnp.bfloat16),
            pltpu.VMEM((2 * STATE, columns), jnp.bfloat16),
        ],
    )
    return pl.pallas_call(
        mix_kernel,
        grid_spec=grid_spec,
        out_shape=jax.ShapeDtypeStruct((frame_count, columns), jnp.bfloat16),
        compiler_params=pltpu.CompilerParams(vmem_limit_bytes=VMEM_BYTES),
        cost_estimate=pl.CostEstimate(
            flops=8 * frame_count * columns * STATE,
            bytes_accessed=4 * frame_count * columns,
            transcendentals=2 * frame_count * heads,
        ),
        name="mix",
    )(slots, frames, proj, logs, skip, entering)


def per_channel(values):
    return jnp.repeat(values, HEAD_DIM, axis=-1)


def enter_states(summary, total_log, shard_count):
    columns = summary.shape[1]
    slices = lax.all_to_all(summary[None], "seq", split_axis=1, concat_axis=0, tiled=True)
    shard_logs = lax.all_gather(total_log[None], "seq", axis=0, tiled=True)
    through = jnp.cumsum(shard_logs, axis=0)
    before_shard = through - shard_logs
    ids = jnp.arange(shard_count)
    earlier = (ids[:, None] > ids[None, :])[:, :, None]
    span = before_shard[:, None, :] - through[None, :, :]
    factors = per_channel(jnp.where(earlier, jnp.exp(jnp.where(earlier, span, 0.0)), 0.0))
    entering = jnp.sum(factors[:, :, None, :] * slices.astype(jnp.float32)[None], axis=1)
    entering = entering.astype(jnp.bfloat16)
    returned = lax.all_to_all(entering, "seq", split_axis=0, concat_axis=1, tiled=True)
    return returned.reshape(STATE, columns)


def shards(shard_count, frames, state_proj, log_decay, skip_gain, group_pos):
    proj = lax.all_gather(state_proj, "head", axis=0, tiled=True)
    groups = group_pos.shape[0]
    heads = skip_gain.shape[0]
    place = group_pos - lax.axis_index("seq") * groups
    slot_ids = jnp.arange(groups, dtype=jnp.int32)
    slots = jnp.sum(jnp.where(place[:, None] == slot_ids[None, :], slot_ids[:, None], 0), axis=0)
    group_log = jnp.sum(log_decay.reshape(heads, groups, GROUP), axis=2)
    onward = group_pos[None, :] >= group_pos[:, None]
    after = jnp.sum(jnp.where(onward[:, None, :], group_log[None], 0.0), axis=2)
    total_log = jnp.sum(group_log, axis=1)
    after = jnp.concatenate([after, after], axis=1)[:, None, :]
    summary = summarise(frames, proj, log_decay, after)
    entering = enter_states(summary, total_log, shard_count)
    skip = per_channel(skip_gain)[None]
    return mix(slots, frames, proj, log_decay, skip, entering)


def solution(mesh):
    return jax.shard_map(
        functools.partial(shards, mesh.shape["seq"]),
        mesh=mesh,
        in_specs=(P("seq", "head"), P("head", "seq"), P("head", "seq"), P("head"), P("seq")),
        out_specs=P("seq", "head"),
        check_vma=False,
    )
```

```python
import functools

import jax
import jax.numpy as jnp
from jax import lax
from jax.experimental import pallas as pl
from jax.experimental.pallas import tpu as pltpu
from jax.sharding import PartitionSpec as P

HEAD_DIM = 64
STATE = 128
GROUP = 256
CHUNK = 128
TILE = 256
PIECES = 2
DECAY_ROWS = 2 * CHUNK + 16
MESH = pl.DeviceIdType.MESH
VMEM_BYTES = 48 * 1024 * 1024


def spread_matrix(heads, columns):
    rows = lax.broadcasted_iota(jnp.int32, (2 * heads, columns), 0) % heads
    owner = lax.broadcasted_iota(jnp.int32, (2 * heads, columns), 1) // HEAD_DIM
    return (rows == owner).astype(jnp.float32).astype(jnp.bfloat16)


def lower_matrix(length):
    rows = lax.broadcasted_iota(jnp.int32, (length, length), 0)
    columns = lax.broadcasted_iota(jnp.int32, (length, length), 1)
    return rows >= columns


def select_sums(mask, values, value_dim):
    high = values.astype(jnp.bfloat16)
    rest = values - high.astype(jnp.float32)
    middle = rest.astype(jnp.bfloat16)
    low = (rest - middle.astype(jnp.float32)).astype(jnp.bfloat16)
    total = None
    for term in (low, middle, high):
        part = lax.dot_general(
            mask, term, (((1,), (value_dim,)), ((), ())), preferred_element_type=jnp.float32
        )
        total = part if total is None else total + part
    return total


def two_terms(values, heads):
    high = values.astype(jnp.bfloat16).astype(jnp.float32)
    lanes = lax.broadcasted_iota(jnp.int32, values.shape, 1)
    return jnp.where(lanes < heads, high, values - high).astype(jnp.bfloat16)


def enter_kernel(
    shard_count,
    head_count,
    frames_ref,
    proj_ref,
    log_ref,
    onward_ref,
    enter_ref,
    input_ref,
    left_ref,
    decay_ref,
    x_ref,
    whole_ref,
    running_ref,
    group_log_ref,
    spread_ref,
    own_ref,
    own_send_ref,
    twin_ref,
    prior_ref,
    next_ref,
    total_ref,
    twin_total_ref,
    rates_ref,
    x_sems,
    proj_send,
    proj_recv,
    twin_send,
    twin_recv,
    next_send,
    next_recv,
    total_sems,
):
    shard = lax.axis_index("seq")
    head = lax.axis_index("head")
    shard_pair, shard_side = shard // 2, shard % 2
    head_pair, head_side = head // 2, head % 2
    shard_pairs, head_pairs = shard_count // 2, head_count // 2
    shard_twin = shard_pair * 2 + 1 - shard_side
    head_twin = head_pair * 2 + 1 - head_side
    has_prior = shard_pair > 0
    has_next = shard_pair < shard_pairs - 1
    shard_prior = jnp.where(has_prior, shard - 2, shard)
    shard_next = jnp.where(has_next, shard + 2, shard)
    frame_count, columns = x_ref.shape
    groups = frame_count // GROUP
    heads = log_ref.shape[0]
    slices = columns // TILE
    piece = frame_count // PIECES

    def read_frames(group):
        rows = pl.ds(pl.multiple_of(group * GROUP, GROUP), GROUP)
        return pltpu.make_async_copy(frames_ref.at[rows], x_ref.at[rows], x_sems.at[group])

    for group in range(groups):
        read_frames(group).start()

    barrier = pltpu.get_barrier_semaphore()

    def greet(device_id):
        pl.semaphore_signal(barrier, inc=1, device_id=device_id, device_id_type=MESH)

    for away in range(1, head_pairs):
        greet({"head": (head_pair + away) % head_pairs * 2 + head_side})
    greet({"head": head_twin})
    greet({"seq": shard_twin})

    @pl.when(has_prior)
    def _():
        greet({"seq": shard_prior})

    @pl.when(has_next)
    def _():
        greet({"seq": shard_next})

    neighbours = head_pairs + 1 + has_prior.astype(jnp.int32) + has_next.astype(jnp.int32)
    pl.semaphore_wait(barrier, neighbours)

    def send_proj(source, owner, target, place, part):
        columns_here = pl.ds(part * piece, piece)
        return pltpu.make_async_remote_copy(
            src_ref=source.at[:, columns_here],
            dst_ref=whole_ref.at[owner, :, columns_here],
            send_sem=proj_send.at[place, part],
            recv_sem=proj_recv.at[owner, part],
            device_id={"head": target},
            device_id_type=MESH,
        )

    proj_copies = []
    for part in range(PIECES):
        for away in range(1, head_pairs):
            target = (head_pair + away) % head_pairs * 2 + head_side
            proj_copies.append(send_proj(proj_ref, head, target, away, part))
            proj_copies[-1].start()
    for part in range(PIECES):
        proj_copies.append(send_proj(proj_ref, head, head_twin, 0, part))
        proj_copies[-1].start()
    whole_ref[head] = proj_ref[...]

    spread_ref[...] = spread_matrix(heads, columns)
    half = CHUNK // 2
    lower = lower_matrix(GROUP).astype(jnp.float32).astype(jnp.bfloat16)

    def sum_group(group, carry):
        frames_here = pl.ds(pl.multiple_of(group * GROUP, GROUP), GROUP)
        logs = log_ref[:, frames_here]
        running = select_sums(lower, jnp.concatenate([logs, logs], axis=0), 1)
        running_ref[frames_here] = running
        group_log_ref[group] = running[GROUP - 1 :]
        for chunk in range(GROUP // CHUNK):
            first = chunk * CHUNK
            here = running[first : first + CHUNK]
            before = running[first - 1 : first] if chunk else jnp.zeros_like(running[:1])
            middle = here[half - 1 : half]
            last = here[CHUNK - 1 :]
            extra = lax.broadcasted_iota(jnp.int32, (16, 2 * heads), 0)
            exponents = jnp.concatenate(
                [
                    middle - here,
                    here - middle,
                    jnp.where(extra == 0, middle - before, last - middle),
                ],
                axis=0,
            )
            decay_ref[group * (GROUP // CHUNK) + chunk] = two_terms(jnp.exp(exponents), heads)
        return carry

    lax.fori_loop(0, groups, sum_group, 0)
    group_logs = jnp.concatenate([group_log_ref[group] for group in range(groups)], axis=0)
    total = jnp.sum(group_logs, axis=0, keepdims=True)
    total_ref[...] = jnp.zeros_like(total_ref)
    total_ref[:, : 2 * heads] = jnp.broadcast_to(total, (8, 2 * heads))
    total_copy = pltpu.make_async_remote_copy(
        src_ref=total_ref,
        dst_ref=twin_total_ref,
        send_sem=total_sems.at[0],
        recv_sem=total_sems.at[1],
        device_id={"seq": shard_twin},
        device_id_type=MESH,
    )
    total_copy.start()
    after = select_sums(onward_ref[...].astype(jnp.bfloat16), group_logs, 0)
    for group in range(groups):
        group_log_ref[group] = after[group : group + 1]

    def scale_group(group, carry):
        read_frames(group).wait()
        rows = pl.ds(pl.multiple_of(group * GROUP, GROUP), GROUP)
        decay = two_terms(jnp.exp(group_log_ref[group] - running_ref[rows]), heads)
        for start in range(0, columns, TILE):
            tile = slice(start, start + TILE)
            wide = jnp.dot(decay, spread_ref[:, tile], preferred_element_type=jnp.float32)
            x_ref[rows, tile] = (x_ref[rows, tile].astype(jnp.float32) * wide).astype(jnp.bfloat16)
        return carry

    lax.fori_loop(0, groups, scale_group, 0)

    for part in range(PIECES):
        for away in range(1, head_pairs):
            owner = (head_pair + away) % head_pairs * 2 + head_side
            send_proj(proj_ref, owner, head_twin, 0, part).wait_recv()
            forward = send_proj(whole_ref.at[owner], owner, head_twin, head_pairs + away - 1, part)
            proj_copies.append(forward)
            forward.start()
    for part in range(PIECES):
        for pair in range(head_pairs):
            owner = pair * 2 + 1 - head_side
            send_proj(proj_ref, owner, head_twin, 0, part).wait_recv()
    rows_each = proj_ref.shape[0]
    for owner in range(head_pairs):
        input_ref[owner * rows_each : (owner + 1) * rows_each] = whole_ref[owner]

    total_copy.wait()
    both_totals = jnp.concatenate([total_ref[:, : 2 * heads], twin_total_ref[:, : 2 * heads]], axis=0)
    rates_ref[...] = jnp.dot(
        two_terms(jnp.exp(both_totals), heads), spread_ref[...], preferred_element_type=jnp.float32
    )

    def twin_copy(index):
        return pltpu.make_async_remote_copy(
            src_ref=own_send_ref.at[index],
            dst_ref=twin_ref.at[index],
            send_sem=twin_send.at[index],
            recv_sem=twin_recv.at[index],
            device_id={"seq": shard_twin},
            device_id_type=MESH,
        )

    def next_copy(index):
        return pltpu.make_async_remote_copy(
            src_ref=next_ref.at[index],
            dst_ref=prior_ref.at[index],
            send_sem=next_send.at[index],
            recv_sem=next_recv.at[index],
            device_id={"seq": shard_next},
            device_id_type=MESH,
        )

    def summarise(index, carry):
        tile = pl.ds(pl.multiple_of(index * TILE, TILE), TILE)
        own = jnp.dot(input_ref[...], x_ref[:, tile], preferred_element_type=jnp.float32)
        own_ref[index] = own
        own_send_ref[index] = own.astype(jnp.bfloat16)
        twin_copy(index).start()
        return carry

    lax.fori_loop(0, slices, summarise, 0)

    @pl.when(jnp.logical_not(has_prior))
    def _():
        prior_ref[...] = jnp.zeros_like(prior_ref)

    causal = lower_matrix(CHUNK)
    chunks = frame_count // CHUNK

    def couple(chunk, carry):
        frames_here = pl.ds(pl.multiple_of(chunk * CHUNK, CHUNK), CHUNK)
        output_rows = whole_ref[head_pairs:, :, frames_here].reshape(STATE, CHUNK)
        output_map = output_rows.astype(jnp.float32).T.astype(jnp.bfloat16)
        coupling = jnp.dot(
            output_map, input_ref[:, frames_here], preferred_element_type=jnp.float32
        )
        left_ref[chunk, :, :CHUNK] = jnp.where(causal, coupling, 0.0).astype(jnp.bfloat16)
        left_ref[chunk, :, CHUNK:] = output_map
        return carry

    first_side = shard_side == 0

    def hand_on(index, carry):
        tile = pl.ds(pl.multiple_of(index * TILE, TILE), TILE)
        own_rate = rates_ref[0:1, tile]
        twin_rate = rates_ref[8:9, tile]
        twin_copy(index).wait_recv()

        @pl.when(has_prior)
        def _():
            next_copy(index).wait_recv()

        own = own_ref[index]
        twin = twin_ref[index].astype(jnp.float32)
        prior = prior_ref[index].astype(jnp.float32)

        @pl.when(has_next)
        def _():
            pair_sum = jnp.where(first_side, twin_rate * own + twin, own_rate * twin + own)
            next_ref[index] = (own_rate * twin_rate * prior + pair_sum).astype(jnp.bfloat16)
            next_copy(index).start()

        enter_ref[:, tile] = jnp.where(first_side, prior, twin_rate * prior + twin).astype(
            jnp.bfloat16
        )
        lax.fori_loop(chunks * index // slices, chunks * (index + 1) // slices, couple, 0)
        return carry

    lax.fori_loop(0, slices, hand_on, 0)

    def finish(index, carry):
        twin_copy(index).wait_send()

        @pl.when(has_next)
        def _():
            next_copy(index).wait_send()

        return carry

    lax.fori_loop(0, slices, finish, 0)
    for copy in proj_copies:
        copy.wait_send()


def enter_states(shard_count, head_count, frames, state_proj, logs, onward):
    frame_count, columns = frames.shape
    heads = logs.shape[0]
    groups = frame_count // GROUP
    chunks = frame_count // CHUNK
    slices = columns // TILE
    vmem = pl.BlockSpec(memory_space=pltpu.VMEM)
    dma = pltpu.SemaphoreType.DMA
    return pl.pallas_call(
        functools.partial(enter_kernel, shard_count, head_count),
        in_specs=[pl.BlockSpec(memory_space=pl.ANY), vmem, vmem, vmem],
        out_specs=[vmem] * 4,
        out_shape=[
            jax.ShapeDtypeStruct((STATE, columns), jnp.bfloat16),
            jax.ShapeDtypeStruct((STATE, frame_count), jnp.bfloat16),
            jax.ShapeDtypeStruct((chunks, CHUNK, 2 * CHUNK), jnp.bfloat16),
            jax.ShapeDtypeStruct((chunks, DECAY_ROWS, 2 * heads), jnp.bfloat16),
        ],
        scratch_shapes=[
            pltpu.VMEM((frame_count, columns), jnp.bfloat16),
            pltpu.VMEM((head_count,) + state_proj.shape, jnp.bfloat16),
            pltpu.VMEM((frame_count, 2 * heads), jnp.float32),
            pltpu.VMEM((groups, 1, 2 * heads), jnp.float32),
            pltpu.VMEM((2 * heads, columns), jnp.bfloat16),
            pltpu.VMEM((slices, STATE, TILE), jnp.float32),
            pltpu.VMEM((slices, STATE, TILE), jnp.bfloat16),
            pltpu.VMEM((slices, STATE, TILE), jnp.bfloat16),
            pltpu.VMEM((slices, STATE, TILE), jnp.bfloat16),
            pltpu.VMEM((slices, STATE, TILE), jnp.bfloat16),
            pltpu.VMEM((8, 128), jnp.float32),
            pltpu.VMEM((8, 128), jnp.float32),
            pltpu.VMEM((16, columns), jnp.float32),
            dma((groups,)),
            dma((head_count, PIECES)),
            dma((head_count, PIECES)),
            dma((slices,)),
            dma((slices,)),
            dma((slices,)),
            dma((slices,)),
            dma((2,)),
        ],
        compiler_params=pltpu.CompilerParams(
            collective_id=0, has_side_effects=True, vmem_limit_bytes=VMEM_BYTES
        ),
        cost_estimate=pl.CostEstimate(
            flops=4 * frame_count * columns * STATE,
            bytes_accessed=2 * frame_count * columns,
            transcendentals=frame_count * heads,
        ),
        name="enter",
    )(frames, state_proj, logs, onward)


def mix_kernel(
    slot_ref, x_ref, left_ref, input_ref, decay_ref, skip_ref, enter_ref, out_ref, state_ref, spread_ref, both_ref
):
    step = pl.program_id(0)
    columns = x_ref.shape[1]
    heads = columns // HEAD_DIM

    @pl.when(step == 0)
    def _():
        state_ref[...] = enter_ref[...].astype(jnp.float32)
        spread_ref[...] = spread_matrix(heads, columns)

    for chunk in range(GROUP // CHUNK):
        rows = slice(chunk * CHUNK, (chunk + 1) * CHUNK)
        for start in range(0, columns, TILE):
            tile = slice(start, start + TILE)
            wide = jnp.dot(decay_ref[chunk], spread_ref[:, tile], preferred_element_type=jnp.float32)
            x = x_ref[rows, tile].astype(jnp.float32)
            scaled = (x * wide[:CHUNK]).astype(jnp.bfloat16)
            prior = state_ref[:, tile] * wide[2 * CHUNK : 2 * CHUNK + 1]
            both_ref[chunk, :CHUNK, tile] = scaled
            both_ref[chunk, CHUNK:, tile] = prior.astype(jnp.bfloat16)
            mixed = jnp.dot(left_ref[chunk], both_ref[chunk, :, tile], preferred_element_type=jnp.float32)
            out_ref[rows, tile] = (
                mixed * wide[CHUNK : 2 * CHUNK] + skip_ref[:, tile] * x
            ).astype(out_ref.dtype)
            update = jnp.dot(input_ref[:, rows], scaled, preferred_element_type=jnp.float32)
            state_ref[:, tile] = (prior + update) * wide[2 * CHUNK + 1 : 2 * CHUNK + 2]


def mix(slots, frames, left, input_map, decay, skip, entering):
    frame_count, columns = frames.shape
    heads = columns // HEAD_DIM
    groups = frame_count // GROUP
    each = GROUP // CHUNK
    grid_spec = pltpu.PrefetchScalarGridSpec(
        num_scalar_prefetch=1,
        grid=(groups,),
        in_specs=[
            pl.BlockSpec((GROUP, columns), lambda i, slot: (slot[i], 0)),
            pl.BlockSpec((each,) + left.shape[1:], lambda i, slot: (slot[i], 0, 0)),
            pl.BlockSpec((STATE, GROUP), lambda i, slot: (0, slot[i])),
            pl.BlockSpec((each,) + decay.shape[1:], lambda i, slot: (slot[i], 0, 0)),
            pl.BlockSpec((1, columns), lambda i, slot: (0, 0)),
            pl.BlockSpec((STATE, columns), lambda i, slot: (0, 0)),
        ],
        out_specs=pl.BlockSpec((GROUP, columns), lambda i, slot: (i, 0)),
        scratch_shapes=[
            pltpu.VMEM((STATE, columns), jnp.float32),
            pltpu.VMEM((2 * heads, columns), jnp.bfloat16),
            pltpu.VMEM((each, CHUNK + STATE, columns), jnp.bfloat16),
        ],
    )
    return pl.pallas_call(
        mix_kernel,
        grid_spec=grid_spec,
        out_shape=jax.ShapeDtypeStruct((frame_count, columns), jnp.bfloat16),
        compiler_params=pltpu.CompilerParams(vmem_limit_bytes=VMEM_BYTES),
        cost_estimate=pl.CostEstimate(
            flops=8 * frame_count * columns * STATE,
            bytes_accessed=4 * frame_count * columns,
            transcendentals=2 * frame_count * heads,
        ),
        name="mix",
    )(slots, frames, left, input_map, decay, skip, entering)


def shards(shard_count, head_count, frames, state_proj, log_decay, skip_gain, group_pos):
    groups = group_pos.shape[0]
    place = group_pos - lax.axis_index("seq") * groups
    slot_ids = jnp.arange(groups, dtype=jnp.int32)
    slots = jnp.sum(jnp.where(place[:, None] == slot_ids[None, :], slot_ids[:, None], 0), axis=0)
    onward = (group_pos[None, :] >= group_pos[:, None]).astype(jnp.float32)
    entering, input_map, left, decay = enter_states(
        shard_count, head_count, frames, state_proj, log_decay, onward
    )
    skip = jnp.repeat(skip_gain, HEAD_DIM)[None]
    return mix(slots, frames, left, input_map, decay, skip, entering)


def solution(mesh):
    return jax.shard_map(
        functools.partial(shards, mesh.shape["seq"], mesh.shape["head"]),
        mesh=mesh,
        in_specs=(P("seq", "head"), P("head", "seq"), P("head", "seq"), P("head"), P("seq")),
        out_specs=P("seq", "head"),
        check_vma=False,
    )
```

```python
import functools

import jax
import jax.numpy as jnp
from jax import lax
from jax.experimental import pallas as pl
from jax.experimental.pallas import tpu as pltpu
from jax.sharding import PartitionSpec as P

HEAD_DIM = 64
STATE = 128
GROUP = 256
CHUNK = 128
TILE = 256
PIECES = 2
LANES = 128
DECAY_ROWS = 2 * CHUNK + 8
MESH = pl.DeviceIdType.MESH
VMEM_BYTES = 48 * 1024 * 1024


def spread_matrix(heads, columns):
    rows = lax.broadcasted_iota(jnp.int32, (LANES, columns), 0)
    owner = lax.broadcasted_iota(jnp.int32, (LANES, columns), 1) // HEAD_DIM
    same = (rows % heads == owner) & (rows < 2 * heads)
    return same.astype(jnp.float32).astype(jnp.bfloat16)


def widen(values, start):
    first = lax.broadcasted_iota(jnp.int32, values.shape, 1) // HEAD_DIM
    parts = [
        jnp.take_along_axis(values, first + at // HEAD_DIM, axis=1, mode="promise_in_bounds")
        for at in range(start, start + TILE, LANES)
    ]
    return jnp.concatenate(parts, axis=1)


def lower_matrix(length):
    rows = lax.broadcasted_iota(jnp.int32, (length, length), 0)
    columns = lax.broadcasted_iota(jnp.int32, (length, length), 1)
    return rows >= columns


def select_sums(mask, values, value_dim):
    high = values.astype(jnp.bfloat16)
    rest = values - high.astype(jnp.float32)
    middle = rest.astype(jnp.bfloat16)
    low = (rest - middle.astype(jnp.float32)).astype(jnp.bfloat16)
    total = None
    for term in (low, middle, high):
        part = lax.dot_general(
            mask, term, (((1,), (value_dim,)), ((), ())), preferred_element_type=jnp.float32
        )
        total = part if total is None else total + part
    return total


def two_terms(values, heads):
    high = values.astype(jnp.bfloat16).astype(jnp.float32)
    lanes = lax.broadcasted_iota(jnp.int32, values.shape, 1)
    return jnp.where(lanes < heads, high, values - high).astype(jnp.bfloat16)


def enter_kernel(
    shard_count,
    head_count,
    frames_ref,
    proj_ref,
    log_ref,
    onward_ref,
    enter_ref,
    left_ref,
    decay_ref,
    input_ref,
    x_ref,
    whole_ref,
    running_ref,
    group_log_ref,
    spread_ref,
    own_ref,
    own_send_ref,
    twin_ref,
    prior_ref,
    next_ref,
    total_ref,
    twin_total_ref,
    rates_ref,
    x_sems,
    proj_send,
    proj_recv,
    twin_send,
    twin_recv,
    next_send,
    next_recv,
    total_sems,
):
    shard = lax.axis_index("seq")
    head = lax.axis_index("head")
    shard_pair, shard_side = shard // 2, shard % 2
    head_pair, head_side = head // 2, head % 2
    shard_pairs, head_pairs = shard_count // 2, head_count // 2
    shard_twin = shard_pair * 2 + 1 - shard_side
    head_twin = head_pair * 2 + 1 - head_side
    has_prior = shard_pair > 0
    has_next = shard_pair < shard_pairs - 1
    shard_prior = jnp.where(has_prior, shard - 2, shard)
    shard_next = jnp.where(has_next, shard + 2, shard)
    frame_count, columns = x_ref.shape
    groups = frame_count // GROUP
    heads = log_ref.shape[0]
    slices = columns // TILE
    piece = frame_count // PIECES

    def read_frames(group):
        rows = pl.ds(pl.multiple_of(group * GROUP, GROUP), GROUP)
        return pltpu.make_async_copy(frames_ref.at[rows], x_ref.at[rows], x_sems.at[group])

    for group in range(groups):
        read_frames(group).start()

    barrier = pltpu.get_barrier_semaphore()

    def greet(device_id):
        pl.semaphore_signal(barrier, inc=1, device_id=device_id, device_id_type=MESH)

    for away in range(1, head_pairs):
        greet({"head": (head_pair + away) % head_pairs * 2 + head_side})
    greet({"head": head_twin})
    greet({"seq": shard_twin})

    @pl.when(has_prior)
    def _():
        greet({"seq": shard_prior})

    @pl.when(has_next)
    def _():
        greet({"seq": shard_next})

    neighbours = head_pairs + 1 + has_prior.astype(jnp.int32) + has_next.astype(jnp.int32)
    pl.semaphore_wait(barrier, neighbours)

    def send_proj(source, owner, target, place, part):
        columns_here = pl.ds(part * piece, piece)
        return pltpu.make_async_remote_copy(
            src_ref=source.at[:, columns_here],
            dst_ref=whole_ref.at[owner, :, columns_here],
            send_sem=proj_send.at[place, part],
            recv_sem=proj_recv.at[owner, part],
            device_id={"head": target},
            device_id_type=MESH,
        )

    proj_copies = []
    for part in range(PIECES):
        for away in range(1, head_pairs):
            target = (head_pair + away) % head_pairs * 2 + head_side
            proj_copies.append(send_proj(proj_ref, head, target, away, part))
            proj_copies[-1].start()
    for part in range(PIECES):
        proj_copies.append(send_proj(proj_ref, head, head_twin, 0, part))
        proj_copies[-1].start()
    whole_ref[head] = proj_ref[...]

    spread_ref[...] = spread_matrix(heads, columns)
    half = CHUNK // 2
    lower = lower_matrix(GROUP).astype(jnp.float32).astype(jnp.bfloat16)

    def sum_group(group, carry):
        frames_here = pl.ds(pl.multiple_of(group * GROUP, GROUP), GROUP)
        logs = log_ref[:, frames_here]
        running = select_sums(lower, jnp.concatenate([logs] * (LANES // heads), axis=0), 1)
        running_ref[frames_here] = running
        group_log_ref[group] = running[GROUP - 1 :]
        for chunk in range(GROUP // CHUNK):
            first = chunk * CHUNK
            here = running[first : first + CHUNK]
            before = running[first - 1 : first] if chunk else jnp.zeros_like(running[:1])
            middle = here[half - 1 : half]
            last = here[CHUNK - 1 :]
            extra = lax.broadcasted_iota(jnp.int32, (8, LANES), 0)
            exponents = jnp.concatenate(
                [
                    middle - here,
                    here - middle,
                    jnp.where(extra == 0, middle - before, last - middle),
                ],
                axis=0,
            )
            decay_ref[group * (GROUP // CHUNK) + chunk] = jnp.exp(exponents)
        return carry

    lax.fori_loop(0, groups, sum_group, 0)
    group_logs = jnp.concatenate([group_log_ref[group] for group in range(groups)], axis=0)
    total = jnp.sum(group_logs, axis=0, keepdims=True)
    total_ref[...] = jnp.broadcast_to(total, total_ref.shape)
    total_copy = pltpu.make_async_remote_copy(
        src_ref=total_ref,
        dst_ref=twin_total_ref,
        send_sem=total_sems.at[0],
        recv_sem=total_sems.at[1],
        device_id={"seq": shard_twin},
        device_id_type=MESH,
    )
    total_copy.start()
    after = select_sums(onward_ref[...].astype(jnp.bfloat16), group_logs, 0)
    for group in range(groups):
        group_log_ref[group] = after[group : group + 1]

    def scale_group(group, carry):
        read_frames(group).wait()
        rows = pl.ds(pl.multiple_of(group * GROUP, GROUP), GROUP)
        decay = two_terms(jnp.exp(group_log_ref[group] - running_ref[rows]), heads)
        for start in range(0, columns, TILE):
            tile = slice(start, start + TILE)
            wide = jnp.dot(decay, spread_ref[:, tile], preferred_element_type=jnp.float32)
            x_ref[rows, tile] = (x_ref[rows, tile].astype(jnp.float32) * wide).astype(jnp.bfloat16)
        return carry

    lax.fori_loop(0, groups, scale_group, 0)

    for part in range(PIECES):
        for away in range(1, head_pairs):
            owner = (head_pair + away) % head_pairs * 2 + head_side
            send_proj(proj_ref, owner, head_twin, 0, part).wait_recv()
            forward = send_proj(whole_ref.at[owner], owner, head_twin, head_pairs + away - 1, part)
            proj_copies.append(forward)
            forward.start()
    for part in range(PIECES):
        for pair in range(head_pairs):
            owner = pair * 2 + 1 - head_side
            send_proj(proj_ref, owner, head_twin, 0, part).wait_recv()
    rows_each = proj_ref.shape[0]
    for owner in range(head_pairs):
        input_ref[owner * rows_each : (owner + 1) * rows_each] = whole_ref[owner]

    total_copy.wait()
    both_totals = jnp.concatenate([total_ref[...], twin_total_ref[...]], axis=0)
    rates_ref[...] = jnp.dot(
        two_terms(jnp.exp(both_totals), heads), spread_ref[...], preferred_element_type=jnp.float32
    )

    def twin_copy(index):
        return pltpu.make_async_remote_copy(
            src_ref=own_send_ref.at[index],
            dst_ref=twin_ref.at[index],
            send_sem=twin_send.at[index],
            recv_sem=twin_recv.at[index],
            device_id={"seq": shard_twin},
            device_id_type=MESH,
        )

    def next_copy(index):
        return pltpu.make_async_remote_copy(
            src_ref=next_ref.at[index],
            dst_ref=prior_ref.at[index],
            send_sem=next_send.at[index],
            recv_sem=next_recv.at[index],
            device_id={"seq": shard_next},
            device_id_type=MESH,
        )

    def summarise(index, carry):
        tile = pl.ds(pl.multiple_of(index * TILE, TILE), TILE)
        own = jnp.dot(input_ref[...], x_ref[:, tile], preferred_element_type=jnp.float32)
        own_ref[index] = own
        own_send_ref[index] = own.astype(jnp.bfloat16)
        twin_copy(index).start()
        return carry

    lax.fori_loop(0, slices, summarise, 0)

    @pl.when(jnp.logical_not(has_prior))
    def _():
        prior_ref[...] = jnp.zeros_like(prior_ref)

    causal = lower_matrix(CHUNK)
    chunks = frame_count // CHUNK

    def couple(chunk, carry):
        frames_here = pl.ds(pl.multiple_of(chunk * CHUNK, CHUNK), CHUNK)
        output_rows = whole_ref[head_pairs:, :, frames_here].reshape(STATE, CHUNK)
        output_map = output_rows.astype(jnp.float32).T.astype(jnp.bfloat16)
        input_map = input_ref[:, frames_here]
        coupling = jnp.dot(output_map, input_map, preferred_element_type=jnp.float32)
        left_ref[chunk, :CHUNK, :CHUNK] = jnp.where(causal, coupling, 0.0).astype(jnp.bfloat16)
        left_ref[chunk, :CHUNK, CHUNK:] = output_map
        left_ref[chunk, CHUNK:, :CHUNK] = input_map
        left_ref[chunk, CHUNK:, CHUNK:] = jnp.zeros((STATE, STATE), jnp.bfloat16)
        return carry

    first_side = shard_side == 0

    def hand_on(index, carry):
        tile = pl.ds(pl.multiple_of(index * TILE, TILE), TILE)
        own_rate = rates_ref[0:1, tile]
        twin_rate = rates_ref[8:9, tile]
        twin_copy(index).wait_recv()

        @pl.when(has_prior)
        def _():
            next_copy(index).wait_recv()

        own = own_ref[index]
        twin = twin_ref[index].astype(jnp.float32)
        prior = prior_ref[index].astype(jnp.float32)

        @pl.when(has_next)
        def _():
            pair_sum = jnp.where(first_side, twin_rate * own + twin, own_rate * twin + own)
            next_ref[index] = (own_rate * twin_rate * prior + pair_sum).astype(jnp.bfloat16)
            next_copy(index).start()

        enter_ref[:, tile] = jnp.where(first_side, prior, twin_rate * prior + twin).astype(
            jnp.bfloat16
        )
        lax.fori_loop(chunks * index // slices, chunks * (index + 1) // slices, couple, 0)
        return carry

    lax.fori_loop(0, slices, hand_on, 0)

    def finish(index, carry):
        twin_copy(index).wait_send()

        @pl.when(has_next)
        def _():
            next_copy(index).wait_send()

        return carry

    lax.fori_loop(0, slices, finish, 0)
    for copy in proj_copies:
        copy.wait_send()


def enter_states(shard_count, head_count, frames, state_proj, logs, onward):
    frame_count, columns = frames.shape
    heads = logs.shape[0]
    groups = frame_count // GROUP
    chunks = frame_count // CHUNK
    slices = columns // TILE
    vmem = pl.BlockSpec(memory_space=pltpu.VMEM)
    dma = pltpu.SemaphoreType.DMA
    return pl.pallas_call(
        functools.partial(enter_kernel, shard_count, head_count),
        in_specs=[pl.BlockSpec(memory_space=pl.ANY), vmem, vmem, vmem],
        out_specs=[vmem] * 3,
        out_shape=[
            jax.ShapeDtypeStruct((STATE, columns), jnp.bfloat16),
            jax.ShapeDtypeStruct((chunks, CHUNK + STATE, CHUNK + STATE), jnp.bfloat16),
            jax.ShapeDtypeStruct((chunks, DECAY_ROWS, LANES), jnp.float32),
        ],
        scratch_shapes=[
            pltpu.VMEM((STATE, frame_count), jnp.bfloat16),
            pltpu.VMEM((frame_count, columns), jnp.bfloat16),
            pltpu.VMEM((head_count,) + state_proj.shape, jnp.bfloat16),
            pltpu.VMEM((frame_count, LANES), jnp.float32),
            pltpu.VMEM((groups, 1, LANES), jnp.float32),
            pltpu.VMEM((LANES, columns), jnp.bfloat16),
            pltpu.VMEM((slices, STATE, TILE), jnp.float32),
            pltpu.VMEM((slices, STATE, TILE), jnp.bfloat16),
            pltpu.VMEM((slices, STATE, TILE), jnp.bfloat16),
            pltpu.VMEM((slices, STATE, TILE), jnp.bfloat16),
            pltpu.VMEM((slices, STATE, TILE), jnp.bfloat16),
            pltpu.VMEM((8, 128), jnp.float32),
            pltpu.VMEM((8, 128), jnp.float32),
            pltpu.VMEM((16, columns), jnp.float32),
            dma((groups,)),
            dma((head_count, PIECES)),
            dma((head_count, PIECES)),
            dma((slices,)),
            dma((slices,)),
            dma((slices,)),
            dma((slices,)),
            dma((2,)),
        ],
        compiler_params=pltpu.CompilerParams(
            collective_id=0, has_side_effects=True, vmem_limit_bytes=VMEM_BYTES
        ),
        cost_estimate=pl.CostEstimate(
            flops=4 * frame_count * columns * STATE,
            bytes_accessed=2 * frame_count * columns,
            transcendentals=frame_count * heads,
        ),
        name="enter",
    )(frames, state_proj, logs, onward)


def mix_kernel(slot_ref, x_ref, left_ref, decay_ref, skip_ref, enter_ref, out_ref, state_ref):
    step = pl.program_id(0)
    columns = x_ref.shape[1]

    @pl.when(step == 0)
    def _():
        state_ref[...] = enter_ref[...].astype(jnp.float32)

    for chunk in range(GROUP // CHUNK):
        rows = slice(chunk * CHUNK, (chunk + 1) * CHUNK)
        for start in range(0, columns, TILE):
            tile = slice(start, start + TILE)
            x = x_ref[rows, tile].astype(jnp.float32)
            scaled = x * widen(decay_ref[chunk, :CHUNK], start)
            ends = widen(decay_ref[chunk, 2 * CHUNK :], start)
            prior = state_ref[:, tile] * ends[0:1]
            both = jnp.concatenate([scaled.astype(jnp.bfloat16), prior.astype(jnp.bfloat16)], axis=0)
            sums = jnp.dot(left_ref[chunk], both, preferred_element_type=jnp.float32)
            mixed = sums[:CHUNK] * widen(decay_ref[chunk, CHUNK : 2 * CHUNK], start)
            out_ref[rows, tile] = (mixed + skip_ref[:, tile] * x).astype(out_ref.dtype)
            state_ref[:, tile] = (prior + sums[CHUNK:]) * ends[1:2]


def mix(slots, frames, left, decay, skip, entering):
    frame_count, columns = frames.shape
    heads = columns // HEAD_DIM
    groups = frame_count // GROUP
    each = GROUP // CHUNK
    grid_spec = pltpu.PrefetchScalarGridSpec(
        num_scalar_prefetch=1,
        grid=(groups,),
        in_specs=[
            pl.BlockSpec((GROUP, columns), lambda i, slot: (slot[i], 0)),
            pl.BlockSpec((each,) + left.shape[1:], lambda i, slot: (slot[i], 0, 0)),
            pl.BlockSpec((each,) + decay.shape[1:], lambda i, slot: (slot[i], 0, 0)),
            pl.BlockSpec((1, columns), lambda i, slot: (0, 0)),
            pl.BlockSpec((STATE, columns), lambda i, slot: (0, 0)),
        ],
        out_specs=pl.BlockSpec((GROUP, columns), lambda i, slot: (i, 0)),
        scratch_shapes=[
            pltpu.VMEM((STATE, columns), jnp.float32),
        ],
    )
    return pl.pallas_call(
        mix_kernel,
        grid_spec=grid_spec,
        out_shape=jax.ShapeDtypeStruct((frame_count, columns), jnp.bfloat16),
        compiler_params=pltpu.CompilerParams(vmem_limit_bytes=VMEM_BYTES),
        cost_estimate=pl.CostEstimate(
            flops=8 * frame_count * columns * STATE,
            bytes_accessed=4 * frame_count * columns,
            transcendentals=2 * frame_count * heads,
        ),
        name="mix",
    )(slots, frames, left, decay, skip, entering)


def shards(shard_count, head_count, frames, state_proj, log_decay, skip_gain, group_pos):
    groups = group_pos.shape[0]
    place = group_pos - lax.axis_index("seq") * groups
    slot_ids = jnp.arange(groups, dtype=jnp.int32)
    slots = jnp.sum(jnp.where(place[:, None] == slot_ids[None, :], slot_ids[:, None], 0), axis=0)
    onward = (group_pos[None, :] >= group_pos[:, None]).astype(jnp.float32)
    entering, left, decay = enter_states(
        shard_count, head_count, frames, state_proj, log_decay, onward
    )
    skip = jnp.repeat(skip_gain, HEAD_DIM)[None]
    return mix(slots, frames, left, decay, skip, entering)


def solution(mesh):
    return jax.shard_map(
        functools.partial(shards, mesh.shape["seq"], mesh.shape["head"]),
        mesh=mesh,
        in_specs=(P("seq", "head"), P("head", "seq"), P("head", "seq"), P("head"), P("seq")),
        out_specs=P("seq", "head"),
        check_vma=False,
    )
```

```python
import functools

import jax
import jax.numpy as jnp
from jax import lax
from jax.experimental import pallas as pl
from jax.experimental.pallas import tpu as pltpu
from jax.sharding import PartitionSpec as P

HEAD_DIM = 64
STATE = 128
GROUP = 256
CHUNK = 128
TILE = 256
PIECES = 2
LANES = 128
DECAY_ROWS = 2 * CHUNK + 8
MESH = pl.DeviceIdType.MESH
VMEM_BYTES = 48 * 1024 * 1024


def spread_matrix(heads, columns):
    rows = lax.broadcasted_iota(jnp.int32, (LANES, columns), 0)
    owner = lax.broadcasted_iota(jnp.int32, (LANES, columns), 1) // HEAD_DIM
    same = (rows % heads == owner) & (rows < 2 * heads)
    return same.astype(jnp.float32).astype(jnp.bfloat16)


def widen(values, start):
    first = lax.broadcasted_iota(jnp.int32, values.shape, 1) // HEAD_DIM
    parts = [
        jnp.take_along_axis(values, first + at // HEAD_DIM, axis=1, mode="promise_in_bounds")
        for at in range(start, start + TILE, LANES)
    ]
    return jnp.concatenate(parts, axis=1)


def lower_matrix(length):
    rows = lax.broadcasted_iota(jnp.int32, (length, length), 0)
    columns = lax.broadcasted_iota(jnp.int32, (length, length), 1)
    return rows >= columns


def select_sums(mask, values, value_dim):
    high = values.astype(jnp.bfloat16)
    rest = values - high.astype(jnp.float32)
    middle = rest.astype(jnp.bfloat16)
    low = (rest - middle.astype(jnp.float32)).astype(jnp.bfloat16)
    total = None
    for term in (low, middle, high):
        part = lax.dot_general(
            mask, term, (((1,), (value_dim,)), ((), ())), preferred_element_type=jnp.float32
        )
        total = part if total is None else total + part
    return total


def two_terms(values, heads):
    high = values.astype(jnp.bfloat16).astype(jnp.float32)
    lanes = lax.broadcasted_iota(jnp.int32, values.shape, 1)
    return jnp.where(lanes < heads, high, values - high).astype(jnp.bfloat16)


def enter_kernel(
    shard_count,
    head_count,
    frames_ref,
    proj_ref,
    log_ref,
    onward_ref,
    enter_ref,
    left_ref,
    decay_ref,
    input_ref,
    x_ref,
    whole_ref,
    running_ref,
    leave_ref,
    spread_ref,
    own_ref,
    own_send_ref,
    twin_ref,
    prior_ref,
    next_ref,
    total_ref,
    twin_total_ref,
    rates_ref,
    x_sems,
    proj_send,
    proj_recv,
    twin_send,
    twin_recv,
    next_send,
    next_recv,
    total_sems,
):
    shard = lax.axis_index("seq")
    head = lax.axis_index("head")
    shard_pair, shard_side = shard // 2, shard % 2
    head_pair, head_side = head // 2, head % 2
    shard_pairs, head_pairs = shard_count // 2, head_count // 2
    shard_twin = shard_pair * 2 + 1 - shard_side
    head_twin = head_pair * 2 + 1 - head_side
    has_prior = shard_pair > 0
    has_next = shard_pair < shard_pairs - 1
    shard_prior = jnp.where(has_prior, shard - 2, shard)
    shard_next = jnp.where(has_next, shard + 2, shard)
    frame_count, columns = x_ref.shape
    groups = frame_count // GROUP
    heads = log_ref.shape[0]
    slices = columns // TILE
    piece = frame_count // PIECES

    def read_frames(group):
        rows = pl.ds(pl.multiple_of(group * GROUP, GROUP), GROUP)
        return pltpu.make_async_copy(frames_ref.at[rows], x_ref.at[rows], x_sems.at[group])

    for group in range(groups):
        read_frames(group).start()

    barrier = pltpu.get_barrier_semaphore()

    def greet(device_id):
        pl.semaphore_signal(barrier, inc=1, device_id=device_id, device_id_type=MESH)

    for away in range(1, head_pairs):
        greet({"head": (head_pair + away) % head_pairs * 2 + head_side})
    greet({"head": head_twin})
    greet({"seq": shard_twin})

    @pl.when(has_prior)
    def _():
        greet({"seq": shard_prior})

    @pl.when(has_next)
    def _():
        greet({"seq": shard_next})

    neighbours = head_pairs + 1 + has_prior.astype(jnp.int32) + has_next.astype(jnp.int32)
    pl.semaphore_wait(barrier, neighbours)

    def send_proj(source, owner, target, place, part):
        columns_here = pl.ds(part * piece, piece)
        return pltpu.make_async_remote_copy(
            src_ref=source.at[:, columns_here],
            dst_ref=whole_ref.at[owner, :, columns_here],
            send_sem=proj_send.at[place, part],
            recv_sem=proj_recv.at[owner, part],
            device_id={"head": target},
            device_id_type=MESH,
        )

    proj_copies = []
    for part in range(PIECES):
        for away in range(1, head_pairs):
            target = (head_pair + away) % head_pairs * 2 + head_side
            proj_copies.append(send_proj(proj_ref, head, target, away, part))
            proj_copies[-1].start()
    for part in range(PIECES):
        proj_copies.append(send_proj(proj_ref, head, head_twin, 0, part))
        proj_copies[-1].start()
    whole_ref[head] = proj_ref[...]

    spread_ref[...] = spread_matrix(heads, columns)
    lower = lower_matrix(GROUP).astype(jnp.float32).astype(jnp.bfloat16)

    group_rows = [slice(group * GROUP, (group + 1) * GROUP) for group in range(groups)]
    for rows in group_rows:
        logs = log_ref[:, rows]
        running_ref[rows] = select_sums(lower, jnp.concatenate([logs] * (LANES // heads), axis=0), 1)
    group_logs = jnp.concatenate([running_ref[rows.stop - 1 : rows.stop] for rows in group_rows], axis=0)
    total = jnp.sum(group_logs, axis=0, keepdims=True)
    total_ref[...] = jnp.broadcast_to(total, total_ref.shape)
    total_copy = pltpu.make_async_remote_copy(
        src_ref=total_ref,
        dst_ref=twin_total_ref,
        send_sem=total_sems.at[0],
        recv_sem=total_sems.at[1],
        device_id={"seq": shard_twin},
        device_id_type=MESH,
    )
    total_copy.start()
    after = select_sums(onward_ref[...].astype(jnp.bfloat16), group_logs, 0)
    for group, rows in enumerate(group_rows):
        leaving = jnp.exp(after[group : group + 1] - running_ref[rows])
        leave_ref[rows] = two_terms(leaving, heads)

    for part in range(PIECES):
        for away in range(1, head_pairs):
            owner = (head_pair + away) % head_pairs * 2 + head_side
            send_proj(proj_ref, owner, head_twin, 0, part).wait_recv()
            forward = send_proj(whole_ref.at[owner], owner, head_twin, head_pairs + away - 1, part)
            proj_copies.append(forward)
            forward.start()
    for part in range(PIECES):
        for pair in range(head_pairs):
            owner = pair * 2 + 1 - head_side
            send_proj(proj_ref, owner, head_twin, 0, part).wait_recv()
    rows_each = proj_ref.shape[0]
    for owner in range(head_pairs):
        input_ref[owner * rows_each : (owner + 1) * rows_each] = whole_ref[owner]

    total_copy.wait()
    both_totals = jnp.concatenate([total_ref[...], twin_total_ref[...]], axis=0)
    rates_ref[...] = jnp.dot(
        two_terms(jnp.exp(both_totals), heads), spread_ref[...], preferred_element_type=jnp.float32
    )

    def twin_copy(index):
        return pltpu.make_async_remote_copy(
            src_ref=own_send_ref.at[index],
            dst_ref=twin_ref.at[index],
            send_sem=twin_send.at[index],
            recv_sem=twin_recv.at[index],
            device_id={"seq": shard_twin},
            device_id_type=MESH,
        )

    def next_copy(index):
        return pltpu.make_async_remote_copy(
            src_ref=next_ref.at[index],
            dst_ref=prior_ref.at[index],
            send_sem=next_send.at[index],
            recv_sem=next_recv.at[index],
            device_id={"seq": shard_next},
            device_id_type=MESH,
        )

    def summarise(index):
        tile = pl.ds(pl.multiple_of(index * TILE, TILE), TILE)
        own = None
        for rows in group_rows:
            wide = jnp.dot(leave_ref[rows], spread_ref[:, tile], preferred_element_type=jnp.float32)
            carried = (x_ref[rows, tile].astype(jnp.float32) * wide).astype(jnp.bfloat16)
            part = jnp.dot(input_ref[:, rows], carried, preferred_element_type=jnp.float32)
            own = part if own is None else own + part
        own_ref[index] = own
        own_send_ref[index] = own.astype(jnp.bfloat16)
        twin_copy(index).start()

    for group in range(groups):
        read_frames(group).wait()

    @pl.when(jnp.logical_not(has_prior))
    def _():
        prior_ref[...] = jnp.zeros_like(prior_ref)

    causal = lower_matrix(CHUNK)
    half = CHUNK // 2
    batch = 2 if groups % 2 == 0 else 1

    def couple_chunk(chunk, first_chunk):
        frames_here = pl.ds(pl.multiple_of(chunk * CHUNK, CHUNK), CHUNK)
        output_rows = whole_ref[head_pairs:, :, frames_here].reshape(STATE, CHUNK)
        output_map = output_rows.astype(jnp.float32).T.astype(jnp.bfloat16)
        input_map = input_ref[:, frames_here]
        coupling = jnp.dot(output_map, input_map, preferred_element_type=jnp.float32)
        left_ref[chunk, :CHUNK, :CHUNK] = jnp.where(causal, coupling, 0.0).astype(jnp.bfloat16)
        left_ref[chunk, :CHUNK, CHUNK:] = output_map
        left_ref[chunk, CHUNK:, :CHUNK] = input_map
        left_ref[chunk, CHUNK:, CHUNK:] = jnp.zeros((STATE, STATE), jnp.bfloat16)
        here = running_ref[frames_here]
        middle = here[half - 1 : half]
        last = here[CHUNK - 1 :]
        if first_chunk:
            before = jnp.zeros_like(last)
        else:
            eight = pl.ds(pl.multiple_of(chunk * CHUNK - 8, 8), 8)
            before = running_ref[eight][7:]
        extra = lax.broadcasted_iota(jnp.int32, (8, LANES), 0)
        decay_ref[chunk, :CHUNK] = jnp.exp(middle - here)
        decay_ref[chunk, CHUNK : 2 * CHUNK] = jnp.exp(here - middle)
        decay_ref[chunk, 2 * CHUNK :] = jnp.exp(
            jnp.where(extra == 0, middle - before, last - middle)
        )

    def couple(index, carry):
        each = GROUP // CHUNK
        for place in range(batch * each):
            couple_chunk(index * (batch * each) + place, place % each == 0)
        return carry

    first_side = shard_side == 0

    def hand_on(index):
        tile = pl.ds(pl.multiple_of(index * TILE, TILE), TILE)
        own_rate = rates_ref[0:1, tile]
        twin_rate = rates_ref[8:9, tile]
        twin_copy(index).wait_recv()

        @pl.when(has_prior)
        def _():
            next_copy(index).wait_recv()

        own = own_ref[index]
        twin = twin_ref[index].astype(jnp.float32)
        prior = prior_ref[index].astype(jnp.float32)

        @pl.when(has_next)
        def _():
            pair_sum = jnp.where(first_side, twin_rate * own + twin, own_rate * twin + own)
            next_ref[index] = (own_rate * twin_rate * prior + pair_sum).astype(jnp.bfloat16)
            next_copy(index).start()

        enter_ref[:, tile] = jnp.where(first_side, prior, twin_rate * prior + twin).astype(
            jnp.bfloat16
        )

    lag = jnp.where(has_next, jnp.minimum(2 + 2 * shard_pair, slices), slices)

    def advance(step, carry):
        @pl.when(step < slices)
        def _():
            summarise(step)

        @pl.when((step == slices - 1) & jnp.logical_not(has_next))
        def _():
            lax.fori_loop(0, groups // batch, couple, 0)

        @pl.when(step >= lag)
        def _():
            hand_on(step - lag)

        return carry

    lax.fori_loop(0, slices + lag, advance, 0)

    @pl.when(has_next)
    def _():
        lax.fori_loop(0, groups // batch, couple, 0)

    def finish(index, carry):
        twin_copy(index).wait_send()

        @pl.when(has_next)
        def _():
            next_copy(index).wait_send()

        return carry

    lax.fori_loop(0, slices, finish, 0)
    for copy in proj_copies:
        copy.wait_send()


def enter_states(shard_count, head_count, frames, state_proj, logs, onward):
    frame_count, columns = frames.shape
    heads = logs.shape[0]
    groups = frame_count // GROUP
    chunks = frame_count // CHUNK
    slices = columns // TILE
    vmem = pl.BlockSpec(memory_space=pltpu.VMEM)
    dma = pltpu.SemaphoreType.DMA
    return pl.pallas_call(
        functools.partial(enter_kernel, shard_count, head_count),
        in_specs=[pl.BlockSpec(memory_space=pl.ANY), vmem, vmem, vmem],
        out_specs=[vmem] * 3,
        out_shape=[
            jax.ShapeDtypeStruct((STATE, columns), jnp.bfloat16),
            jax.ShapeDtypeStruct((chunks, CHUNK + STATE, CHUNK + STATE), jnp.bfloat16),
            jax.ShapeDtypeStruct((chunks, DECAY_ROWS, LANES), jnp.float32),
        ],
        scratch_shapes=[
            pltpu.VMEM((STATE, frame_count), jnp.bfloat16),
            pltpu.VMEM((frame_count, columns), jnp.bfloat16),
            pltpu.VMEM((head_count,) + state_proj.shape, jnp.bfloat16),
            pltpu.VMEM((frame_count, LANES), jnp.float32),
            pltpu.VMEM((frame_count, LANES), jnp.bfloat16),
            pltpu.VMEM((LANES, columns), jnp.bfloat16),
            pltpu.VMEM((slices, STATE, TILE), jnp.float32),
            pltpu.VMEM((slices, STATE, TILE), jnp.bfloat16),
            pltpu.VMEM((slices, STATE, TILE), jnp.bfloat16),
            pltpu.VMEM((slices, STATE, TILE), jnp.bfloat16),
            pltpu.VMEM((slices, STATE, TILE), jnp.bfloat16),
            pltpu.VMEM((8, 128), jnp.float32),
            pltpu.VMEM((8, 128), jnp.float32),
            pltpu.VMEM((16, columns), jnp.float32),
            dma((groups,)),
            dma((head_count, PIECES)),
            dma((head_count, PIECES)),
            dma((slices,)),
            dma((slices,)),
            dma((slices,)),
            dma((slices,)),
            dma((2,)),
        ],
        compiler_params=pltpu.CompilerParams(
            collective_id=0, has_side_effects=True, vmem_limit_bytes=VMEM_BYTES
        ),
        cost_estimate=pl.CostEstimate(
            flops=4 * frame_count * columns * STATE,
            bytes_accessed=2 * frame_count * columns,
            transcendentals=frame_count * heads,
        ),
        name="enter",
    )(frames, state_proj, logs, onward)


def mix_kernel(slot_ref, x_ref, left_ref, decay_ref, skip_ref, enter_ref, out_ref, state_ref):
    step = pl.program_id(0)
    columns = x_ref.shape[1]

    @pl.when(step == 0)
    def _():
        state_ref[...] = enter_ref[...].astype(jnp.float32)

    for chunk in range(GROUP // CHUNK):
        rows = slice(chunk * CHUNK, (chunk + 1) * CHUNK)
        for start in range(0, columns, TILE):
            tile = slice(start, start + TILE)
            x = x_ref[rows, tile].astype(jnp.float32)
            scaled = x * widen(decay_ref[chunk, :CHUNK], start)
            ends = widen(decay_ref[chunk, 2 * CHUNK :], start)
            prior = state_ref[:, tile] * ends[0:1]
            both = jnp.concatenate([scaled.astype(jnp.bfloat16), prior.astype(jnp.bfloat16)], axis=0)
            sums = jnp.dot(left_ref[chunk], both, preferred_element_type=jnp.float32)
            mixed = sums[:CHUNK] * widen(decay_ref[chunk, CHUNK : 2 * CHUNK], start)
            out_ref[rows, tile] = (mixed + skip_ref[:, tile] * x).astype(out_ref.dtype)
            state_ref[:, tile] = (prior + sums[CHUNK:]) * ends[1:2]


def mix(slots, frames, left, decay, skip, entering):
    frame_count, columns = frames.shape
    heads = columns // HEAD_DIM
    groups = frame_count // GROUP
    each = GROUP // CHUNK
    grid_spec = pltpu.PrefetchScalarGridSpec(
        num_scalar_prefetch=1,
        grid=(groups,),
        in_specs=[
            pl.BlockSpec((GROUP, columns), lambda i, slot: (slot[i], 0)),
            pl.BlockSpec((each,) + left.shape[1:], lambda i, slot: (slot[i], 0, 0)),
            pl.BlockSpec((each,) + decay.shape[1:], lambda i, slot: (slot[i], 0, 0)),
            pl.BlockSpec((1, columns), lambda i, slot: (0, 0)),
            pl.BlockSpec((STATE, columns), lambda i, slot: (0, 0)),
        ],
        out_specs=pl.BlockSpec((GROUP, columns), lambda i, slot: (i, 0)),
        scratch_shapes=[
            pltpu.VMEM((STATE, columns), jnp.float32),
        ],
    )
    return pl.pallas_call(
        mix_kernel,
        grid_spec=grid_spec,
        out_shape=jax.ShapeDtypeStruct((frame_count, columns), jnp.bfloat16),
        compiler_params=pltpu.CompilerParams(vmem_limit_bytes=VMEM_BYTES),
        cost_estimate=pl.CostEstimate(
            flops=8 * frame_count * columns * STATE,
            bytes_accessed=4 * frame_count * columns,
            transcendentals=2 * frame_count * heads,
        ),
        name="mix",
    )(slots, frames, left, decay, skip, entering)


def shards(shard_count, head_count, frames, state_proj, log_decay, skip_gain, group_pos):
    groups = group_pos.shape[0]
    place = group_pos - lax.axis_index("seq") * groups
    slot_ids = jnp.arange(groups, dtype=jnp.int32)
    slots = jnp.sum(jnp.where(place[:, None] == slot_ids[None, :], slot_ids[:, None], 0), axis=0)
    onward = (group_pos[None, :] >= group_pos[:, None]).astype(jnp.float32)
    entering, left, decay = enter_states(
        shard_count, head_count, frames, state_proj, log_decay, onward
    )
    skip = jnp.repeat(skip_gain, HEAD_DIM)[None]
    return mix(slots, frames, left, decay, skip, entering)


def solution(mesh):
    return jax.shard_map(
        functools.partial(shards, mesh.shape["seq"], mesh.shape["head"]),
        mesh=mesh,
        in_specs=(P("seq", "head"), P("head", "seq"), P("head", "seq"), P("head"), P("seq")),
        out_specs=P("seq", "head"),
        check_vma=False,
    )
```

```python
import functools

import jax
import jax.numpy as jnp
from jax import lax
from jax.experimental import pallas as pl
from jax.experimental.pallas import tpu as pltpu
from jax.sharding import PartitionSpec as P

HEAD_DIM = 64
STATE = 128
GROUP = 256
CHUNK = 128
TILE = 256
PIECES = 2
LANES = 128
MESH = pl.DeviceIdType.MESH
VMEM_BYTES = 48 * 1024 * 1024


def spread_matrix(heads, columns):
    rows = lax.broadcasted_iota(jnp.int32, (LANES, columns), 0)
    owner = lax.broadcasted_iota(jnp.int32, (LANES, columns), 1) // HEAD_DIM
    same = (rows % heads == owner) & (rows < 2 * heads)
    return same.astype(jnp.float32).astype(jnp.bfloat16)


def lower_matrix(length):
    rows = lax.broadcasted_iota(jnp.int32, (length, length), 0)
    columns = lax.broadcasted_iota(jnp.int32, (length, length), 1)
    return rows >= columns


def select_sums(mask, values, value_dim):
    high = values.astype(jnp.bfloat16)
    rest = values - high.astype(jnp.float32)
    middle = rest.astype(jnp.bfloat16)
    low = (rest - middle.astype(jnp.float32)).astype(jnp.bfloat16)
    total = None
    for term in (low, middle, high):
        part = lax.dot_general(
            mask, term, (((1,), (value_dim,)), ((), ())), preferred_element_type=jnp.float32
        )
        total = part if total is None else total + part
    return total


def two_terms(values, heads):
    high = values.astype(jnp.bfloat16).astype(jnp.float32)
    lanes = lax.broadcasted_iota(jnp.int32, values.shape, 1)
    return jnp.where(lanes < heads, high, values - high).astype(jnp.bfloat16)


def enter_kernel(
    shard_count,
    head_count,
    frames_ref,
    proj_ref,
    log_ref,
    onward_ref,
    enter_ref,
    left_ref,
    decay_ref,
    input_ref,
    x_ref,
    whole_ref,
    running_ref,
    leave_ref,
    spread_ref,
    own_ref,
    own_send_ref,
    twin_ref,
    prior_ref,
    next_ref,
    total_ref,
    twin_total_ref,
    rates_ref,
    x_sems,
    proj_send,
    proj_recv,
    twin_send,
    twin_recv,
    next_send,
    next_recv,
    total_sems,
):
    shard = lax.axis_index("seq")
    head = lax.axis_index("head")
    shard_pair, shard_side = shard // 2, shard % 2
    head_pair, head_side = head // 2, head % 2
    shard_pairs, head_pairs = shard_count // 2, head_count // 2
    shard_twin = shard_pair * 2 + 1 - shard_side
    head_twin = head_pair * 2 + 1 - head_side
    has_prior = shard_pair > 0
    has_next = shard_pair < shard_pairs - 1
    shard_prior = jnp.where(has_prior, shard - 2, shard)
    shard_next = jnp.where(has_next, shard + 2, shard)
    frame_count, columns = x_ref.shape
    groups = frame_count // GROUP
    heads = log_ref.shape[0]
    slices = columns // TILE
    piece = frame_count // PIECES

    def read_frames(group):
        rows = pl.ds(pl.multiple_of(group * GROUP, GROUP), GROUP)
        return pltpu.make_async_copy(frames_ref.at[rows], x_ref.at[rows], x_sems.at[group])

    for group in range(groups):
        read_frames(group).start()

    barrier = pltpu.get_barrier_semaphore()

    def greet(device_id):
        pl.semaphore_signal(barrier, inc=1, device_id=device_id, device_id_type=MESH)

    for away in range(1, head_pairs):
        greet({"head": (head_pair + away) % head_pairs * 2 + head_side})
    greet({"head": head_twin})
    greet({"seq": shard_twin})

    @pl.when(has_prior)
    def _():
        greet({"seq": shard_prior})

    @pl.when(has_next)
    def _():
        greet({"seq": shard_next})

    neighbours = head_pairs + 1 + has_prior.astype(jnp.int32) + has_next.astype(jnp.int32)
    pl.semaphore_wait(barrier, neighbours)

    def send_proj(source, owner, target, place, part):
        columns_here = pl.ds(part * piece, piece)
        return pltpu.make_async_remote_copy(
            src_ref=source.at[:, columns_here],
            dst_ref=whole_ref.at[owner, :, columns_here],
            send_sem=proj_send.at[place, part],
            recv_sem=proj_recv.at[owner, part],
            device_id={"head": target},
            device_id_type=MESH,
        )

    proj_copies = []
    for part in range(PIECES):
        for away in range(1, head_pairs):
            target = (head_pair + away) % head_pairs * 2 + head_side
            proj_copies.append(send_proj(proj_ref, head, target, away, part))
            proj_copies[-1].start()
    for part in range(PIECES):
        proj_copies.append(send_proj(proj_ref, head, head_twin, 0, part))
        proj_copies[-1].start()
    whole_ref[head] = proj_ref[...]

    spread_ref[...] = spread_matrix(heads, columns)
    lower = lower_matrix(GROUP).astype(jnp.float32).astype(jnp.bfloat16)

    group_rows = [slice(group * GROUP, (group + 1) * GROUP) for group in range(groups)]
    for rows in group_rows:
        logs = log_ref[:, rows]
        running_ref[rows] = select_sums(lower, jnp.concatenate([logs] * (LANES // heads), axis=0), 1)
    group_logs = jnp.concatenate([running_ref[rows.stop - 1 : rows.stop] for rows in group_rows], axis=0)
    total = jnp.sum(group_logs, axis=0, keepdims=True)
    total_ref[...] = jnp.broadcast_to(total, total_ref.shape)
    total_copy = pltpu.make_async_remote_copy(
        src_ref=total_ref,
        dst_ref=twin_total_ref,
        send_sem=total_sems.at[0],
        recv_sem=total_sems.at[1],
        device_id={"seq": shard_twin},
        device_id_type=MESH,
    )
    total_copy.start()
    after = select_sums(onward_ref[...].astype(jnp.bfloat16), group_logs, 0)
    for group, rows in enumerate(group_rows):
        leaving = jnp.exp(after[group : group + 1] - running_ref[rows])
        leave_ref[rows] = two_terms(leaving, heads)

    for part in range(PIECES):
        for away in range(1, head_pairs):
            owner = (head_pair + away) % head_pairs * 2 + head_side
            send_proj(proj_ref, owner, head_twin, 0, part).wait_recv()
            forward = send_proj(whole_ref.at[owner], owner, head_twin, head_pairs + away - 1, part)
            proj_copies.append(forward)
            forward.start()
    for part in range(PIECES):
        for pair in range(head_pairs):
            owner = pair * 2 + 1 - head_side
            send_proj(proj_ref, owner, head_twin, 0, part).wait_recv()
    rows_each = proj_ref.shape[0]
    for owner in range(head_pairs):
        input_ref[owner * rows_each : (owner + 1) * rows_each] = whole_ref[owner]

    total_copy.wait()
    both_totals = jnp.concatenate([total_ref[...], twin_total_ref[...]], axis=0)
    rates_ref[...] = jnp.dot(
        two_terms(jnp.exp(both_totals), heads), spread_ref[...], preferred_element_type=jnp.float32
    )

    def twin_copy(index):
        return pltpu.make_async_remote_copy(
            src_ref=own_send_ref.at[index],
            dst_ref=twin_ref.at[index],
            send_sem=twin_send.at[index],
            recv_sem=twin_recv.at[index],
            device_id={"seq": shard_twin},
            device_id_type=MESH,
        )

    def next_copy(index):
        return pltpu.make_async_remote_copy(
            src_ref=next_ref.at[index],
            dst_ref=prior_ref.at[index],
            send_sem=next_send.at[index],
            recv_sem=next_recv.at[index],
            device_id={"seq": shard_next},
            device_id_type=MESH,
        )

    def summarise(index):
        tile = pl.ds(pl.multiple_of(index * TILE, TILE), TILE)
        own = None
        for rows in group_rows:
            wide = jnp.dot(leave_ref[rows], spread_ref[:, tile], preferred_element_type=jnp.float32)
            carried = (x_ref[rows, tile].astype(jnp.float32) * wide).astype(jnp.bfloat16)
            part = jnp.dot(input_ref[:, rows], carried, preferred_element_type=jnp.float32)
            own = part if own is None else own + part
        own_ref[index] = own
        own_send_ref[index] = own.astype(jnp.bfloat16)
        twin_copy(index).start()

    for group in range(groups):
        read_frames(group).wait()

    @pl.when(jnp.logical_not(has_prior))
    def _():
        prior_ref[...] = jnp.zeros_like(prior_ref)

    causal = lower_matrix(CHUNK)
    half = CHUNK // 2
    batch = 2 if groups % 2 == 0 else 1
    causal_terms = causal.astype(jnp.float32).astype(jnp.bfloat16)
    frame_ids = lax.broadcasted_iota(jnp.int32, (CHUNK, CHUNK), 1)
    onto = lax.broadcasted_iota(jnp.int32, (CHUNK, CHUNK), 0) <= frame_ids

    def couple_chunk(chunk):
        frames_here = pl.ds(pl.multiple_of(chunk * CHUNK, CHUNK), CHUNK)
        output_map = whole_ref[head_pairs:, :, frames_here].reshape(STATE, CHUNK)
        input_map = input_ref[:, frames_here].astype(jnp.float32).T.astype(jnp.bfloat16)
        coupling = jnp.dot(input_map, output_map, preferred_element_type=jnp.float32)
        left_ref[chunk, :CHUNK, :CHUNK] = jnp.where(onto, coupling, 0.0).astype(jnp.bfloat16)
        left_ref[chunk, :CHUNK, CHUNK:] = input_map
        left_ref[chunk, CHUNK:, :CHUNK] = output_map
        left_ref[chunk, CHUNK:, CHUNK:] = jnp.zeros((STATE, STATE), jnp.bfloat16)
        logs = log_ref[:, frames_here]
        high = logs.astype(jnp.bfloat16)
        rest = logs - high.astype(jnp.float32)
        nearer = rest.astype(jnp.bfloat16)
        low = (rest - nearer.astype(jnp.float32)).astype(jnp.bfloat16)
        here = None
        for term in (low, nearer, high):
            part = lax.dot_general(
                term, causal_terms, (((1,), (1,)), ((), ())), preferred_element_type=jnp.float32
            )
            here = part if here is None else here + part
        middle = here[:, half - 1 : half]
        last = here[:, CHUNK - 1 :]
        decay_ref[chunk, :heads] = jnp.exp(middle - here)
        decay_ref[chunk, heads : 2 * heads] = jnp.exp(here - middle)
        decay_ref[chunk, 2 * heads : 3 * heads] = jnp.exp(jnp.broadcast_to(middle, here.shape))
        decay_ref[chunk, 3 * heads :] = jnp.exp(jnp.broadcast_to(last - middle, here.shape))

    def couple(index, carry):
        each = GROUP // CHUNK
        for place in range(batch * each):
            couple_chunk(index * (batch * each) + place)
        return carry

    first_side = shard_side == 0

    def hand_on(index):
        tile = pl.ds(pl.multiple_of(index * TILE, TILE), TILE)
        own_rate = rates_ref[0:1, tile]
        twin_rate = rates_ref[8:9, tile]
        twin_copy(index).wait_recv()

        @pl.when(has_prior)
        def _():
            next_copy(index).wait_recv()

        own = own_ref[index]
        twin = twin_ref[index].astype(jnp.float32)
        prior = prior_ref[index].astype(jnp.float32)

        @pl.when(has_next)
        def _():
            pair_sum = jnp.where(first_side, twin_rate * own + twin, own_rate * twin + own)
            next_ref[index] = (own_rate * twin_rate * prior + pair_sum).astype(jnp.bfloat16)
            next_copy(index).start()

        enter_ref[:, tile] = jnp.where(first_side, prior, twin_rate * prior + twin).astype(
            jnp.bfloat16
        )

    lag = jnp.where(has_next, jnp.minimum(2 + 2 * shard_pair, slices), slices)

    def advance(step, carry):
        @pl.when(step < slices)
        def _():
            summarise(step)

        @pl.when((step == slices - 1) & jnp.logical_not(has_next))
        def _():
            lax.fori_loop(0, groups // batch, couple, 0)

        @pl.when(step >= lag)
        def _():
            hand_on(step - lag)

        return carry

    lax.fori_loop(0, slices + lag, advance, 0)

    @pl.when(has_next)
    def _():
        lax.fori_loop(0, groups // batch, couple, 0)

    def finish(index, carry):
        twin_copy(index).wait_send()

        @pl.when(has_next)
        def _():
            next_copy(index).wait_send()

        return carry

    lax.fori_loop(0, slices, finish, 0)
    for copy in proj_copies:
        copy.wait_send()


def enter_states(shard_count, head_count, frames, state_proj, logs, onward):
    frame_count, columns = frames.shape
    heads = logs.shape[0]
    groups = frame_count // GROUP
    chunks = frame_count // CHUNK
    slices = columns // TILE
    vmem = pl.BlockSpec(memory_space=pltpu.VMEM)
    dma = pltpu.SemaphoreType.DMA
    return pl.pallas_call(
        functools.partial(enter_kernel, shard_count, head_count),
        in_specs=[pl.BlockSpec(memory_space=pl.ANY), vmem, vmem, vmem],
        out_specs=[vmem] * 3,
        out_shape=[
            jax.ShapeDtypeStruct((STATE, columns), jnp.bfloat16),
            jax.ShapeDtypeStruct((chunks, CHUNK + STATE, CHUNK + STATE), jnp.bfloat16),
            jax.ShapeDtypeStruct((chunks, 4 * heads, CHUNK), jnp.float32),
        ],
        scratch_shapes=[
            pltpu.VMEM((STATE, frame_count), jnp.bfloat16),
            pltpu.VMEM((frame_count, columns), jnp.bfloat16),
            pltpu.VMEM((head_count,) + state_proj.shape, jnp.bfloat16),
            pltpu.VMEM((frame_count, LANES), jnp.float32),
            pltpu.VMEM((frame_count, LANES), jnp.bfloat16),
            pltpu.VMEM((LANES, columns), jnp.bfloat16),
            pltpu.VMEM((slices, STATE, TILE), jnp.float32),
            pltpu.VMEM((slices, STATE, TILE), jnp.bfloat16),
            pltpu.VMEM((slices, STATE, TILE), jnp.bfloat16),
            pltpu.VMEM((slices, STATE, TILE), jnp.bfloat16),
            pltpu.VMEM((slices, STATE, TILE), jnp.bfloat16),
            pltpu.VMEM((8, 128), jnp.float32),
            pltpu.VMEM((8, 128), jnp.float32),
            pltpu.VMEM((16, columns), jnp.float32),
            dma((groups,)),
            dma((head_count, PIECES)),
            dma((head_count, PIECES)),
            dma((slices,)),
            dma((slices,)),
            dma((slices,)),
            dma((slices,)),
            dma((2,)),
        ],
        compiler_params=pltpu.CompilerParams(
            collective_id=0, has_side_effects=True, vmem_limit_bytes=VMEM_BYTES
        ),
        cost_estimate=pl.CostEstimate(
            flops=4 * frame_count * columns * STATE,
            bytes_accessed=2 * frame_count * columns,
            transcendentals=frame_count * heads,
        ),
        name="enter",
    )(frames, state_proj, logs, onward)


def mix_kernel(slot_ref, x_ref, left_ref, decay_ref, skip_ref, enter_ref, out_ref, state_ref):
    step = pl.program_id(0)
    columns = x_ref.shape[1]
    heads = columns // HEAD_DIM

    @pl.when(step == 0)
    def _():
        for start in range(0, columns, TILE):
            tile = slice(start, start + TILE)
            state_ref[tile] = enter_ref[:, tile].astype(jnp.float32).T

    for chunk in range(GROUP // CHUNK):
        rows = slice(chunk * CHUNK, (chunk + 1) * CHUNK)
        for start in range(0, columns, TILE):
            tile = slice(start, start + TILE)
            heads_here = range(start // HEAD_DIM, (start + TILE) // HEAD_DIM)

            def spread(ref, first):
                return jnp.concatenate(
                    [
                        jnp.broadcast_to(ref[first + head : first + head + 1], (HEAD_DIM, CHUNK))
                        for head in heads_here
                    ],
                    axis=0,
                )

            factors = decay_ref.at[chunk]
            x = x_ref[rows, tile].T.astype(jnp.float32)
            scaled = x * spread(factors, 0)
            prior = state_ref[tile] * spread(factors, 2 * heads)
            both = jnp.concatenate([scaled.astype(jnp.bfloat16), prior.astype(jnp.bfloat16)], axis=1)
            sums = jnp.dot(both, left_ref[chunk], preferred_element_type=jnp.float32)
            mixed = sums[:, :CHUNK] * spread(factors, heads) + spread(skip_ref, 0) * x
            out_ref[rows, tile] = mixed.astype(out_ref.dtype).T
            state_ref[tile] = (prior + sums[:, CHUNK:]) * spread(factors, 3 * heads)


def mix(slots, frames, left, decay, skip, entering):
    frame_count, columns = frames.shape
    heads = columns // HEAD_DIM
    groups = frame_count // GROUP
    each = GROUP // CHUNK
    grid_spec = pltpu.PrefetchScalarGridSpec(
        num_scalar_prefetch=1,
        grid=(groups,),
        in_specs=[
            pl.BlockSpec((GROUP, columns), lambda i, slot: (slot[i], 0)),
            pl.BlockSpec((each,) + left.shape[1:], lambda i, slot: (slot[i], 0, 0)),
            pl.BlockSpec((each,) + decay.shape[1:], lambda i, slot: (slot[i], 0, 0)),
            pl.BlockSpec((heads, CHUNK), lambda i, slot: (0, 0)),
            pl.BlockSpec((STATE, columns), lambda i, slot: (0, 0)),
        ],
        out_specs=pl.BlockSpec((GROUP, columns), lambda i, slot: (i, 0)),
        scratch_shapes=[pltpu.VMEM((columns, STATE), jnp.float32)],
    )
    return pl.pallas_call(
        mix_kernel,
        grid_spec=grid_spec,
        out_shape=jax.ShapeDtypeStruct((frame_count, columns), jnp.bfloat16),
        compiler_params=pltpu.CompilerParams(vmem_limit_bytes=VMEM_BYTES),
        cost_estimate=pl.CostEstimate(
            flops=8 * frame_count * columns * STATE,
            bytes_accessed=4 * frame_count * columns,
            transcendentals=2 * frame_count * heads,
        ),
        name="mix",
    )(slots, frames, left, decay, skip, entering)


def shards(shard_count, head_count, frames, state_proj, log_decay, skip_gain, group_pos):
    groups = group_pos.shape[0]
    place = group_pos - lax.axis_index("seq") * groups
    slot_ids = jnp.arange(groups, dtype=jnp.int32)
    slots = jnp.sum(jnp.where(place[:, None] == slot_ids[None, :], slot_ids[:, None], 0), axis=0)
    onward = (group_pos[None, :] >= group_pos[:, None]).astype(jnp.float32)
    entering, left, decay = enter_states(
        shard_count, head_count, frames, state_proj, log_decay, onward
    )
    skip = jnp.broadcast_to(skip_gain[:, None], (skip_gain.shape[0], CHUNK))
    return mix(slots, frames, left, decay, skip, entering)


def solution(mesh):
    return jax.shard_map(
        functools.partial(shards, mesh.shape["seq"], mesh.shape["head"]),
        mesh=mesh,
        in_specs=(P("seq", "head"), P("head", "seq"), P("head", "seq"), P("head"), P("seq")),
        out_specs=P("seq", "head"),
        check_vma=False,
    )
```

```python
import functools

import jax
import jax.numpy as jnp
from jax import lax
from jax.experimental import pallas as pl
from jax.experimental.pallas import tpu as pltpu
from jax.sharding import PartitionSpec as P

HEAD_DIM = 64
STATE = 128
GROUP = 256
CHUNK = 128
TILE = 256
PIECES = 2
LANES = 128
MESH = pl.DeviceIdType.MESH
VMEM_BYTES = 48 * 1024 * 1024


def lower_matrix(length):
    rows = lax.broadcasted_iota(jnp.int32, (length, length), 0)
    columns = lax.broadcasted_iota(jnp.int32, (length, length), 1)
    return rows >= columns


def select_sums(mask, values, value_dim):
    high = values.astype(jnp.bfloat16)
    rest = values - high.astype(jnp.float32)
    middle = rest.astype(jnp.bfloat16)
    low = (rest - middle.astype(jnp.float32)).astype(jnp.bfloat16)
    total = None
    for term in (low, middle, high):
        part = lax.dot_general(
            mask, term, (((1,), (value_dim,)), ((), ())), preferred_element_type=jnp.float32
        )
        total = part if total is None else total + part
    return total


def row_sums(logs, lower):
    high = logs.astype(jnp.bfloat16)
    rest = logs - high.astype(jnp.float32)
    middle = rest.astype(jnp.bfloat16)
    low = (rest - middle.astype(jnp.float32)).astype(jnp.bfloat16)
    total = None
    for term in (low, middle, high):
        part = lax.dot_general(
            term, lower, (((1,), (1,)), ((), ())), preferred_element_type=jnp.float32
        )
        total = part if total is None else total + part
    return total


def enter_kernel(
    shard_count,
    head_count,
    frames_ref,
    proj_ref,
    log_ref,
    onward_ref,
    enter_ref,
    left_ref,
    decay_ref,
    input_ref,
    x_ref,
    whole_ref,
    leave_ref,
    turned_ref,
    own_ref,
    own_send_ref,
    twin_ref,
    prior_ref,
    next_ref,
    total_ref,
    twin_total_ref,
    rates_ref,
    x_sems,
    proj_send,
    proj_recv,
    twin_send,
    twin_recv,
    next_send,
    next_recv,
    total_sems,
):
    shard = lax.axis_index("seq")
    head = lax.axis_index("head")
    shard_pair, shard_side = shard // 2, shard % 2
    head_pair, head_side = head // 2, head % 2
    shard_pairs, head_pairs = shard_count // 2, head_count // 2
    shard_twin = shard_pair * 2 + 1 - shard_side
    head_twin = head_pair * 2 + 1 - head_side
    has_prior = shard_pair > 0
    has_next = shard_pair < shard_pairs - 1
    shard_prior = jnp.where(has_prior, shard - 2, shard)
    shard_next = jnp.where(has_next, shard + 2, shard)
    frame_count, columns = x_ref.shape
    groups = frame_count // GROUP
    heads = log_ref.shape[0]
    slices = columns // TILE
    piece = frame_count // PIECES

    def read_frames(group):
        rows = pl.ds(pl.multiple_of(group * GROUP, GROUP), GROUP)
        return pltpu.make_async_copy(frames_ref.at[rows], x_ref.at[rows], x_sems.at[group])

    for group in range(groups):
        read_frames(group).start()

    barrier = pltpu.get_barrier_semaphore()

    def greet(device_id):
        pl.semaphore_signal(barrier, inc=1, device_id=device_id, device_id_type=MESH)

    for away in range(1, head_pairs):
        greet({"head": (head_pair + away) % head_pairs * 2 + head_side})
    greet({"head": head_twin})
    greet({"seq": shard_twin})

    @pl.when(has_prior)
    def _():
        greet({"seq": shard_prior})

    @pl.when(has_next)
    def _():
        greet({"seq": shard_next})

    neighbours = head_pairs + 1 + has_prior.astype(jnp.int32) + has_next.astype(jnp.int32)
    pl.semaphore_wait(barrier, neighbours)

    def send_proj(source, owner, target, place, part):
        columns_here = pl.ds(part * piece, piece)
        return pltpu.make_async_remote_copy(
            src_ref=source.at[:, columns_here],
            dst_ref=whole_ref.at[owner, :, columns_here],
            send_sem=proj_send.at[place, part],
            recv_sem=proj_recv.at[owner, part],
            device_id={"head": target},
            device_id_type=MESH,
        )

    proj_copies = []
    for part in range(PIECES):
        for away in range(1, head_pairs):
            target = (head_pair + away) % head_pairs * 2 + head_side
            proj_copies.append(send_proj(proj_ref, head, target, away, part))
            proj_copies[-1].start()
    for part in range(PIECES):
        proj_copies.append(send_proj(proj_ref, head, head_twin, 0, part))
        proj_copies[-1].start()
    whole_ref[head] = proj_ref[...]

    lower = lower_matrix(GROUP).astype(jnp.float32).astype(jnp.bfloat16)
    ones = jnp.ones((8, GROUP), jnp.bfloat16)
    group_rows = [slice(group * GROUP, (group + 1) * GROUP) for group in range(groups)]
    group_logs = jnp.concatenate(
        [
            select_sums(ones, jnp.concatenate([log_ref[:, rows]] * (LANES // heads), axis=0), 1)[:1]
            for rows in group_rows
        ],
        axis=0,
    )
    after = select_sums(onward_ref[...].astype(jnp.bfloat16), group_logs, 0).T
    total_ref[...] = jnp.broadcast_to(after[:heads, groups : groups + 1], total_ref.shape)
    total_copy = pltpu.make_async_remote_copy(
        src_ref=total_ref,
        dst_ref=twin_total_ref,
        send_sem=total_sems.at[0],
        recv_sem=total_sems.at[1],
        device_id={"seq": shard_twin},
        device_id_type=MESH,
    )
    total_copy.start()
    for group, rows in enumerate(group_rows):
        running = row_sums(log_ref[:, rows], lower)
        leave_ref[:, rows] = jnp.exp(after[:heads, group : group + 1] - running)

    for part in range(PIECES):
        for away in range(1, head_pairs):
            owner = (head_pair + away) % head_pairs * 2 + head_side
            send_proj(proj_ref, owner, head_twin, 0, part).wait_recv()
            forward = send_proj(whole_ref.at[owner], owner, head_twin, head_pairs + away - 1, part)
            proj_copies.append(forward)
            forward.start()
    for part in range(PIECES):
        for pair in range(head_pairs):
            owner = pair * 2 + 1 - head_side
            send_proj(proj_ref, owner, head_twin, 0, part).wait_recv()
    rows_each = proj_ref.shape[0]
    for owner in range(head_pairs):
        input_ref[owner * rows_each : (owner + 1) * rows_each] = whole_ref[owner]

    total_copy.wait()
    rates_ref[:heads] = jnp.exp(total_ref[...])
    rates_ref[heads:] = jnp.exp(twin_total_ref[...])
    for rows in group_rows:
        turned_ref[rows] = input_ref[:, rows].astype(jnp.float32).T.astype(jnp.bfloat16)
    heads_each = TILE // HEAD_DIM

    def spread(ref, first, lanes):
        return jnp.concatenate(
            [
                jnp.broadcast_to(ref[pl.ds(first + head, 1), lanes], (HEAD_DIM, lanes.stop - lanes.start))
                for head in range(heads_each)
            ],
            axis=0,
        )

    def twin_copy(index):
        return pltpu.make_async_remote_copy(
            src_ref=own_send_ref.at[index],
            dst_ref=twin_ref.at[index],
            send_sem=twin_send.at[index],
            recv_sem=twin_recv.at[index],
            device_id={"seq": shard_twin},
            device_id_type=MESH,
        )

    def next_copy(index):
        return pltpu.make_async_remote_copy(
            src_ref=next_ref.at[index],
            dst_ref=prior_ref.at[index],
            send_sem=next_send.at[index],
            recv_sem=next_recv.at[index],
            device_id={"seq": shard_next},
            device_id_type=MESH,
        )

    def summarise(index):
        tile = pl.ds(pl.multiple_of(index * TILE, TILE), TILE)
        own = None
        for rows in group_rows:
            wide = spread(leave_ref, index * heads_each, rows)
            carried = (x_ref[rows, tile].T.astype(jnp.float32) * wide).astype(jnp.bfloat16)
            part = jnp.dot(carried, turned_ref[rows], preferred_element_type=jnp.float32)
            own = part if own is None else own + part
        own_ref[index] = own
        own_send_ref[index] = own.astype(jnp.bfloat16)
        twin_copy(index).start()

    for group in range(groups):
        read_frames(group).wait()

    @pl.when(jnp.logical_not(has_prior))
    def _():
        prior_ref[...] = jnp.zeros_like(prior_ref)

    causal = lower_matrix(CHUNK)
    half = CHUNK // 2
    batch = 2 if groups % 2 == 0 else 1
    causal_terms = causal.astype(jnp.float32).astype(jnp.bfloat16)
    frame_ids = lax.broadcasted_iota(jnp.int32, (CHUNK, CHUNK), 1)
    onto = lax.broadcasted_iota(jnp.int32, (CHUNK, CHUNK), 0) <= frame_ids

    def couple_chunk(chunk):
        frames_here = pl.ds(pl.multiple_of(chunk * CHUNK, CHUNK), CHUNK)
        output_map = whole_ref[head_pairs:, :, frames_here].reshape(STATE, CHUNK)
        input_map = input_ref[:, frames_here].astype(jnp.float32).T.astype(jnp.bfloat16)
        coupling = jnp.dot(input_map, output_map, preferred_element_type=jnp.float32)
        left_ref[chunk, :CHUNK, :CHUNK] = jnp.where(onto, coupling, 0.0).astype(jnp.bfloat16)
        left_ref[chunk, :CHUNK, CHUNK:] = input_map
        left_ref[chunk, CHUNK:, :CHUNK] = output_map
        left_ref[chunk, CHUNK:, CHUNK:] = jnp.zeros((STATE, STATE), jnp.bfloat16)
        logs = log_ref[:, frames_here]
        here = row_sums(logs, causal_terms)
        middle = here[:, half - 1 : half]
        last = here[:, CHUNK - 1 :]
        decay_ref[chunk, :heads] = jnp.exp(middle - here)
        decay_ref[chunk, heads : 2 * heads] = jnp.exp(here - middle)
        decay_ref[chunk, 2 * heads : 3 * heads] = jnp.exp(jnp.broadcast_to(middle, here.shape))
        decay_ref[chunk, 3 * heads :] = jnp.exp(jnp.broadcast_to(last - middle, here.shape))

    def couple(index, carry):
        each = GROUP // CHUNK
        for place in range(batch * each):
            couple_chunk(index * (batch * each) + place)
        return carry

    first_side = shard_side == 0

    def hand_on(index):
        tile = pl.ds(pl.multiple_of(index * TILE, TILE), TILE)
        own_rate = spread(rates_ref, index * heads_each, slice(0, STATE))
        twin_rate = spread(rates_ref, heads + index * heads_each, slice(0, STATE))
        twin_copy(index).wait_recv()

        @pl.when(has_prior)
        def _():
            next_copy(index).wait_recv()

        own = own_ref[index]
        twin = twin_ref[index].astype(jnp.float32)
        prior = prior_ref[index].astype(jnp.float32)

        @pl.when(has_next)
        def _():
            pair_sum = jnp.where(first_side, twin_rate * own + twin, own_rate * twin + own)
            next_ref[index] = (own_rate * twin_rate * prior + pair_sum).astype(jnp.bfloat16)
            next_copy(index).start()

        enter_ref[tile] = jnp.where(first_side, prior, twin_rate * prior + twin).astype(
            jnp.bfloat16
        )

    lag = jnp.where(has_next, jnp.minimum(2 + 2 * shard_pair, slices), slices)

    def advance(step, carry):
        @pl.when(step < slices)
        def _():
            summarise(step)

        @pl.when((step == slices - 1) & jnp.logical_not(has_next))
        def _():
            lax.fori_loop(0, groups // batch, couple, 0)

        @pl.when(step >= lag)
        def _():
            hand_on(step - lag)

        return carry

    lax.fori_loop(0, slices + lag, advance, 0)

    @pl.when(has_next)
    def _():
        lax.fori_loop(0, groups // batch, couple, 0)

    def finish(index, carry):
        twin_copy(index).wait_send()

        @pl.when(has_next)
        def _():
            next_copy(index).wait_send()

        return carry

    lax.fori_loop(0, slices, finish, 0)
    for copy in proj_copies:
        copy.wait_send()


def enter_states(shard_count, head_count, frames, state_proj, logs, onward):
    frame_count, columns = frames.shape
    heads = logs.shape[0]
    groups = frame_count // GROUP
    chunks = frame_count // CHUNK
    slices = columns // TILE
    vmem = pl.BlockSpec(memory_space=pltpu.VMEM)
    dma = pltpu.SemaphoreType.DMA
    return pl.pallas_call(
        functools.partial(enter_kernel, shard_count, head_count),
        in_specs=[pl.BlockSpec(memory_space=pl.ANY), vmem, vmem, vmem],
        out_specs=[vmem] * 3,
        out_shape=[
            jax.ShapeDtypeStruct((columns, STATE), jnp.bfloat16),
            jax.ShapeDtypeStruct((chunks, CHUNK + STATE, CHUNK + STATE), jnp.bfloat16),
            jax.ShapeDtypeStruct((chunks, 4 * heads, CHUNK), jnp.float32),
        ],
        scratch_shapes=[
            pltpu.VMEM((STATE, frame_count), jnp.bfloat16),
            pltpu.VMEM((frame_count, columns), jnp.bfloat16),
            pltpu.VMEM((head_count,) + state_proj.shape, jnp.bfloat16),
            pltpu.VMEM((heads, frame_count), jnp.float32),
            pltpu.VMEM((frame_count, STATE), jnp.bfloat16),
            pltpu.VMEM((slices, TILE, STATE), jnp.float32),
            pltpu.VMEM((slices, TILE, STATE), jnp.bfloat16),
            pltpu.VMEM((slices, TILE, STATE), jnp.bfloat16),
            pltpu.VMEM((slices, TILE, STATE), jnp.bfloat16),
            pltpu.VMEM((slices, TILE, STATE), jnp.bfloat16),
            pltpu.VMEM((heads, STATE), jnp.float32),
            pltpu.VMEM((heads, STATE), jnp.float32),
            pltpu.VMEM((2 * heads, STATE), jnp.float32),
            dma((groups,)),
            dma((head_count, PIECES)),
            dma((head_count, PIECES)),
            dma((slices,)),
            dma((slices,)),
            dma((slices,)),
            dma((slices,)),
            dma((2,)),
        ],
        compiler_params=pltpu.CompilerParams(
            collective_id=0, has_side_effects=True, vmem_limit_bytes=VMEM_BYTES
        ),
        cost_estimate=pl.CostEstimate(
            flops=4 * frame_count * columns * STATE,
            bytes_accessed=2 * frame_count * columns,
            transcendentals=frame_count * heads,
        ),
        name="enter",
    )(frames, state_proj, logs, onward)


def mix_kernel(slot_ref, x_ref, left_ref, decay_ref, skip_ref, enter_ref, out_ref, state_ref):
    step = pl.program_id(0)
    columns = x_ref.shape[1]
    heads = columns // HEAD_DIM

    @pl.when(step == 0)
    def _():
        state_ref[...] = enter_ref[...].astype(jnp.float32)

    for chunk in range(GROUP // CHUNK):
        rows = slice(chunk * CHUNK, (chunk + 1) * CHUNK)
        for start in range(0, columns, TILE):
            tile = slice(start, start + TILE)
            heads_here = range(start // HEAD_DIM, (start + TILE) // HEAD_DIM)

            def spread(ref, first):
                return jnp.concatenate(
                    [
                        jnp.broadcast_to(ref[first + head : first + head + 1], (HEAD_DIM, CHUNK))
                        for head in heads_here
                    ],
                    axis=0,
                )

            factors = decay_ref.at[chunk]
            x = x_ref[rows, tile].T.astype(jnp.float32)
            scaled = x * spread(factors, 0)
            prior = state_ref[tile] * spread(factors, 2 * heads)
            both = jnp.concatenate([scaled.astype(jnp.bfloat16), prior.astype(jnp.bfloat16)], axis=1)
            sums = jnp.dot(both, left_ref[chunk], preferred_element_type=jnp.float32)
            mixed = sums[:, :CHUNK] * spread(factors, heads) + spread(skip_ref, 0) * x
            out_ref[rows, tile] = mixed.astype(out_ref.dtype).T
            state_ref[tile] = (prior + sums[:, CHUNK:]) * spread(factors, 3 * heads)


def mix(slots, frames, left, decay, skip, entering):
    frame_count, columns = frames.shape
    heads = columns // HEAD_DIM
    groups = frame_count // GROUP
    each = GROUP // CHUNK
    grid_spec = pltpu.PrefetchScalarGridSpec(
        num_scalar_prefetch=1,
        grid=(groups,),
        in_specs=[
            pl.BlockSpec((GROUP, columns), lambda i, slot: (slot[i], 0)),
            pl.BlockSpec((each,) + left.shape[1:], lambda i, slot: (slot[i], 0, 0)),
            pl.BlockSpec((each,) + decay.shape[1:], lambda i, slot: (slot[i], 0, 0)),
            pl.BlockSpec((heads, CHUNK), lambda i, slot: (0, 0)),
            pl.BlockSpec((columns, STATE), lambda i, slot: (0, 0)),
        ],
        out_specs=pl.BlockSpec((GROUP, columns), lambda i, slot: (i, 0)),
        scratch_shapes=[pltpu.VMEM((columns, STATE), jnp.float32)],
    )
    return pl.pallas_call(
        mix_kernel,
        grid_spec=grid_spec,
        out_shape=jax.ShapeDtypeStruct((frame_count, columns), jnp.bfloat16),
        compiler_params=pltpu.CompilerParams(vmem_limit_bytes=VMEM_BYTES),
        cost_estimate=pl.CostEstimate(
            flops=8 * frame_count * columns * STATE,
            bytes_accessed=4 * frame_count * columns,
            transcendentals=2 * frame_count * heads,
        ),
        name="mix",
    )(slots, frames, left, decay, skip, entering)


def shards(shard_count, head_count, frames, state_proj, log_decay, skip_gain, group_pos):
    groups = group_pos.shape[0]
    place = group_pos - lax.axis_index("seq") * groups
    slot_ids = jnp.arange(groups, dtype=jnp.int32)
    slots = jnp.sum(jnp.where(place[:, None] == slot_ids[None, :], slot_ids[:, None], 0), axis=0)
    floor = jnp.concatenate([group_pos, jnp.zeros((1,), group_pos.dtype)])
    onward = (group_pos[None, :] >= floor[:, None]).astype(jnp.float32)
    entering, left, decay = enter_states(
        shard_count, head_count, frames, state_proj, log_decay, onward
    )
    skip = jnp.broadcast_to(skip_gain[:, None], (skip_gain.shape[0], CHUNK))
    return mix(slots, frames, left, decay, skip, entering)


def solution(mesh):
    return jax.shard_map(
        functools.partial(shards, mesh.shape["seq"], mesh.shape["head"]),
        mesh=mesh,
        in_specs=(P("seq", "head"), P("head", "seq"), P("head", "seq"), P("head"), P("seq")),
        out_specs=P("seq", "head"),
        check_vma=False,
    )
```
